32 devices in a mesh: dp: 8 (over y, x, core), pipe: 4 (over z).
Axes of the slice: x: 2, y: 2, z: 4, core: 2. Of those that a mesh axis runs over, the one named last changes fastest.
Arguments:
- fwd_x: bfloat16 [4, 8, 64, 3584], P('pipe', 'dp'), may hold values from -6 to 6
- fwd_q: bfloat16 [4, 8, 64, 3584], P('pipe', 'dp')
- bwd_x: bfloat16 [4, 8, 64, 3584], P('pipe', 'dp'), may hold values from -6 to 6
- bwd_q: bfloat16 [4, 8, 64, 3584], P('pipe', 'dp')
- bwd_dout: bfloat16 [4, 8, 64, 3584], P('pipe', 'dp'), may hold values from -6 to 6
- cache_kv: bfloat16 [4, 8, 1024, 1024], P('pipe', 'dp'), may hold values from -6 to 6
- kv_weight: bfloat16 [4, 3584, 1024], P('pipe', 'dp'), may hold values from -0.09375 to 0.09375
- seg_lengths: int32 [4, 8, 4], P('pipe', 'dp'), may hold values from 1 to 896, as said below
Outputs:
- next_act: bfloat16 [4, 8, 64, 3584], P('pipe', 'dp')
- grad_q: bfloat16 [4, 8, 64, 3584], P('pipe', 'dp')
- prev_grad: bfloat16 [4, 8, 64, 3584], P('pipe', 'dp')
- weight_grad: float32 [4, 3584, 1024], P('pipe', 'dp')
The draws below stay inside these ranges and needn't reach their ends.
Inputs may be any that keep to these rules, and one draw needn't show every extreme that they name: `seg_lengths`: each row holds four lengths that sum to 1024; the first is at least 1; the second lies from 64 to 127 and is 64 in some row of every draw; the third is at most 64 and equals 64 in some row of every draw; the fourth lies from 32 to the third.
All inputs are finite; a program needn't handle non-finite values.
Results may differ from the reference program's by a relative error of at most 0.035.
Values may be sent and summed in bfloat16 or wider, within the bound.
A program may use at most 128 MiB of HBM per device.

```python
import math
import jax
import jax.numpy as jnp
from jax import lax

D = 3584
HQ = 28
HK = 4
HD = 128
SEG = 64
SEQ = 1024
SECTIONS = 4
SEQS = 8


def cache_base(key):
    base = jax.random.normal(key, (SECTIONS, SEQS, SEQ, 2 * HK * HD), jnp.float32)
    return jnp.clip(base, -6.0, 6.0)


def draw_cache_kv(key, part):
    base = cache_base(key)
    return base.astype(jnp.bfloat16)


def draw_fwd_q(key, part):
    key = jax.random.fold_in(key, 11)
    query = jnp.clip(jax.random.normal(key, (SECTIONS, SEQS, SEG, HQ * HD), jnp.float32), -6.0, 6.0)
    return query.astype(jnp.bfloat16)


def draw_bwd_q(key, part):
    key = jax.random.fold_in(key, 13)
    query = jnp.clip(jax.random.normal(key, (SECTIONS, SEQS, SEG, HQ * HD), jnp.float32), -6.0, 6.0)
    return query.astype(jnp.bfloat16)


def draw_seg_lengths(key, part):
    key = jax.random.fold_in(key, 5)
    key_third, key_pick, key_fourth, key_second = jax.random.split(key, 4)
    shape = (SECTIONS, SEQS)
    count = SECTIONS * SEQS
    third = jax.random.randint(key_third, shape, SEG // 2, SEG + 1)
    pick = jax.random.randint(key_pick, (), 0, count)
    other = (pick + 1) % count
    flat_index = jnp.arange(count, dtype=jnp.int32).reshape(shape)
    is_pick = flat_index == pick
    is_other = flat_index == other
    third = jnp.where(is_pick, SEG, third)
    third = jnp.where(is_other, SEG // 2, third)
    spread = jax.random.randint(key_fourth, shape, 0, 1 << 20)
    fourth = SEG // 2 + spread % (third - SEG // 2 + 1)
    fourth = jnp.where(is_pick | is_other, SEG // 2, fourth)
    second = jax.random.randint(key_second, shape, SEG, 2 * SEG)
    second = jnp.where(is_other, SEG, second)
    first = SEQ - second - third - fourth
    return jnp.stack([first, second, third, fourth], axis=-1).astype(jnp.int32)


def spiked(drawn, rng, source, target, shards_of, factor):
    def block_of(axis_at):
        return (jnp.arange(drawn.shape[axis_at]) // (drawn.shape[axis_at] // shards_of)).reshape((-1,) + (1,) * (drawn.ndim - 1 - axis_at))

    first = jax.random.permutation(rng, shards_of)[block_of(target)]
    far = (block_of(target) + shards_of // 2) % shards_of
    return jnp.where((block_of(source) == first) | (block_of(source) == far), factor * drawn, drawn)


def block_levels(key, shape, cuts, smallest, top_value):
    loudness = 1.0
    for position, shards_of in cuts:
        heights = jax.random.uniform(jax.random.fold_in(jax.random.fold_in(key, 6), position), (shards_of,), jnp.float32, smallest / len(cuts), top_value / len(cuts))
        loudness = loudness * jnp.repeat(jnp.exp(heights), shape[position] // shards_of).reshape((-1,) + (1,) * (len(shape) - 1 - position))
    return loudness


def noise(rng, shape, width, reach, cuts=(), kind=jnp.bfloat16):
    entries = width * jax.random.normal(rng, shape, jnp.float32)
    if cuts:
        entries = entries * block_levels(rng, shape, cuts, -0.22, 0.18)
    return jnp.clip(entries, -reach, reach).astype(kind)


def gaussian_with(rng, shape, scale, reach, shards, heavy, held_as=jnp.bfloat16):
    values = scale * jax.random.normal(rng, shape, jnp.float32)
    if shards:
        values = values * block_levels(rng, shape, shards, -0.22, 0.18)
    return jnp.clip(spiked(values, jax.random.fold_in(rng, 3), *heavy), -reach, reach).astype(held_as)


def setup_inputs(seed: int = 0) -> dict:
    splits = jax.random.split(jax.random.key(seed), 9)
    fwd_x = noise(splits[0], (SECTIONS, SEQS, SEG, D), 1.0, 6.0, ((0, 4), (1, 8)))
    fwd_q = draw_fwd_q(jax.random.fold_in(splits[8], 71), 0)
    bwd_x = gaussian_with(splits[2], (SECTIONS, SEQS, SEG, D), 1.0, 6.0, ((0, 4), (1, 8)), (1, 3, 8, 2.0))
    bwd_q = draw_bwd_q(jax.random.fold_in(splits[8], 71), 0)
    bwd_dout = noise(splits[4], (SECTIONS, SEQS, SEG, HQ * HD), 1.0, 6.0, ((0, 4), (1, 8)))
    cache_kv = draw_cache_kv(jax.random.fold_in(splits[8], 71), 0)
    kv_weight = noise(splits[6], (SECTIONS, D, 2 * HK * HD), D ** -0.5, 0.09375, ((0, 4), (1, 8)))
    seg_lengths = draw_seg_lengths(jax.random.fold_in(splits[8], 71), 0)
    return {"fwd_x": fwd_x, "fwd_q": fwd_q, "bwd_x": bwd_x, "bwd_q": bwd_q, "bwd_dout": bwd_dout, "cache_kv": cache_kv, "kv_weight": kv_weight, "seg_lengths": seg_lengths}


def masked_softmax(scores, allowed):
    masked = jnp.where(allowed[:, None, :], scores, -1e+30)
    top = lax.optimization_barrier(jnp.max(masked, axis=-1, keepdims=True))
    raised = jnp.exp(masked - top)
    return raised / lax.optimization_barrier(jnp.sum(raised, axis=-1, keepdims=True))

def forward_segment(query, own_kv, cache, length):
    seg = query.shape[0]
    seq_len = cache.shape[0]
    half = cache.shape[1] // 2
    kv_heads = half // HD
    group = query.shape[1] // half
    scale = 1.0 / math.sqrt(HD)
    start = (seq_len - length).astype(jnp.int32)
    rows = jnp.arange(seg, dtype=jnp.int32)
    cache_ok = jnp.broadcast_to(jnp.arange(seq_len, dtype=jnp.int32)[None, :] < start, (seg, seq_len))
    own_ok = (rows[None, :] <= rows[:, None]) & (rows[None, :] < length)
    allowed = jnp.concatenate([cache_ok, own_ok], axis=1)
    keys = jnp.concatenate([cache[:, :half], own_kv[:, :half]], axis=0)
    values = jnp.concatenate([cache[:, half:], own_kv[:, half:]], axis=0)
    pieces = []
    for head in range(kv_heads):
        block = query[:, head * group * HD:(head + 1) * group * HD].reshape(seg * group, HD)
        key_head = keys[:, head * HD:(head + 1) * HD]
        scores = (jnp.dot(block, key_head.T, preferred_element_type=jnp.float32) * scale).reshape(seg, group, -1)
        probs = masked_softmax(scores, allowed).astype(jnp.bfloat16).reshape(seg * group, -1)
        mixed = jnp.dot(probs, values[:, head * HD:(head + 1) * HD], preferred_element_type=jnp.float32)
        pieces.append(mixed.reshape(seg, group * HD))
    result = jnp.concatenate(pieces, axis=1)
    return jnp.where((rows < length)[:, None], result, 0.0).astype(jnp.bfloat16)

def backward_segment(query, dout, cache, third, fourth):
    seg = query.shape[0]
    seq_len = cache.shape[0]
    half = cache.shape[1] // 2
    kv_heads = half // HD
    group = query.shape[1] // half
    scale = 1.0 / math.sqrt(HD)
    start = (seq_len - fourth - third).astype(jnp.int32)
    rows = jnp.arange(seg, dtype=jnp.int32)
    allowed = jnp.arange(seq_len, dtype=jnp.int32)[None, :] <= start + rows[:, None]
    live = (rows < third)[:, None]
    dout = jnp.where(live, dout, jnp.zeros_like(dout))
    query_parts, key_parts, value_parts = ([], [], [])
    for head in range(kv_heads):
        block = query[:, head * group * HD:(head + 1) * group * HD].reshape(seg * group, HD)
        grad_block = dout[:, head * group * HD:(head + 1) * group * HD].reshape(seg * group, HD)
        key_head = cache[:, head * HD:(head + 1) * HD]
        value_head = cache[:, half + head * HD:half + (head + 1) * HD]
        scores = (jnp.dot(block, key_head.T, preferred_element_type=jnp.float32) * scale).reshape(seg, group, seq_len)
        probs = masked_softmax(scores, allowed).reshape(seg * group, seq_len)
        rounded = probs.astype(jnp.bfloat16)
        mixed = jnp.dot(rounded, value_head, preferred_element_type=jnp.float32)
        delta = lax.optimization_barrier(jnp.sum(grad_block.astype(jnp.float32) * mixed, axis=1, keepdims=True))
        along = jnp.dot(grad_block, value_head.T, preferred_element_type=jnp.float32)
        dscore = (probs * (along - delta)).astype(jnp.bfloat16)
        query_parts.append((jnp.dot(dscore, key_head, preferred_element_type=jnp.float32) * scale).reshape(seg, group * HD))
        dscore_own = lax.dynamic_slice_in_dim(dscore, start, seg, 1)
        rounded_own = lax.dynamic_slice_in_dim(rounded, start, seg, 1)
        key_parts.append(jnp.dot(dscore_own.T, block, preferred_element_type=jnp.float32) * scale)
        value_parts.append(jnp.dot(rounded_own.T, grad_block, preferred_element_type=jnp.float32))
    grad_query = jnp.concatenate(query_parts, axis=1).astype(jnp.bfloat16)
    kv_grad = jnp.concatenate(key_parts + value_parts, axis=1)
    kv_grad = jnp.where(live, kv_grad, 0.0).astype(jnp.bfloat16)
    return (grad_query, kv_grad)

def reference(fwd_x, fwd_q, bwd_x, bwd_q, bwd_dout, cache_kv, kv_weight, seg_lengths):

    def section(items):
        section_fx, section_fq, section_bx, section_bq, section_dout, section_cache, weight, section_lengths = items

        def one(total, item):
            fx_seq, fq_seq, bx_seq, bq_seq, dout_seq, cache_seq, lengths_seq = item
            own_kv = jnp.dot(fx_seq, weight, preferred_element_type=jnp.float32).astype(jnp.bfloat16)
            fwd_out = forward_segment(fq_seq, own_kv, cache_seq, lengths_seq[3])
            grad_query, kv_grad = backward_segment(bq_seq, dout_seq, cache_seq, lengths_seq[2], lengths_seq[3])
            input_grad = jnp.dot(kv_grad, weight.T, preferred_element_type=jnp.float32).astype(jnp.bfloat16)
            total = total + jnp.dot(bx_seq.T, kv_grad, preferred_element_type=jnp.float32)
            return (total, (fwd_out, grad_query, input_grad))
        empty = jnp.zeros((weight.shape[0], weight.shape[1]), jnp.float32)
        return lax.scan(one, empty, (section_fx, section_fq, section_bx, section_bq, section_dout, section_cache, section_lengths))
    weight_grad, (fwd_out, grad_q, input_grad) = lax.map(section, (fwd_x, fwd_q, bwd_x, bwd_q, bwd_dout, cache_kv, kv_weight, seg_lengths))
    next_act = jnp.concatenate([jnp.zeros_like(fwd_out[:1]), fwd_out[:-1]], axis=0)
    prev_grad = jnp.concatenate([input_grad[1:], jnp.zeros_like(input_grad[:1])], axis=0)
    return (next_act, grad_q, prev_grad, weight_grad)
```

```python
import functools
import math

import jax
import jax.numpy as jnp
from jax import lax
from jax.experimental import pallas as pl
from jax.experimental.pallas import tpu as pltpu
from jax.sharding import PartitionSpec as P

HD = 128


def shifted(value, axis, steps):
    count = lax.axis_size(axis)
    first, last = (max(0, -steps), min(count, count - steps))
    return lax.ppermute(value, axis, [(source, source + steps) for source in range(first, last)])


def masked_softmax(scores, allowed):
    masked = jnp.where(allowed[:, None, :], scores, -1e30)
    top = jnp.max(masked, axis=-1, keepdims=True)
    raised = jnp.exp(masked - top)
    return raised / jnp.sum(raised, axis=-1, keepdims=True)


def forward_segment(query, own_kv, cache, length):
    seg = query.shape[0]
    seq_len = cache.shape[0]
    half = cache.shape[1] // 2
    kv_heads = half // HD
    group = query.shape[1] // half
    scale = 1.0 / math.sqrt(HD)
    start = seq_len - length
    rows = jnp.arange(seg, dtype=jnp.int32)
    cache_ok = jnp.broadcast_to(
        jnp.arange(seq_len, dtype=jnp.int32)[None, :] < start, (seg, seq_len)
    )
    own_ok = (rows[None, :] <= rows[:, None]) & (rows[None, :] < length)
    allowed = jnp.concatenate([cache_ok, own_ok], axis=1)
    keys = jnp.concatenate([cache[:, :half], own_kv[:, :half]], axis=0)
    values = jnp.concatenate([cache[:, half:], own_kv[:, half:]], axis=0)
    pieces = []
    for head in range(kv_heads):
        block = query[:, head * group * HD : (head + 1) * group * HD].reshape(seg * group, HD)
        key_head = keys[:, head * HD : (head + 1) * HD]
        scores = (jnp.dot(block, key_head.T, preferred_element_type=jnp.float32) * scale).reshape(
            seg, group, -1
        )
        probs = masked_softmax(scores, allowed).astype(jnp.bfloat16).reshape(seg * group, -1)
        mixed = jnp.dot(
            probs, values[:, head * HD : (head + 1) * HD], preferred_element_type=jnp.float32
        )
        pieces.append(mixed.reshape(seg, group * HD))
    result = jnp.concatenate(pieces, axis=1)
    return jnp.where((rows < length)[:, None], result, 0.0).astype(jnp.bfloat16)


def backward_segment(query, dout, cache, third, fourth):
    seg = query.shape[0]
    seq_len = cache.shape[0]
    half = cache.shape[1] // 2
    kv_heads = half // HD
    group = query.shape[1] // half
    scale = 1.0 / math.sqrt(HD)
    start = seq_len - fourth - third
    rows = jnp.arange(seg, dtype=jnp.int32)
    allowed = jnp.arange(seq_len, dtype=jnp.int32)[None, :] <= start + rows[:, None]
    live = (rows < third)[:, None]
    dout = jnp.where(live, dout, jnp.zeros_like(dout))
    query_parts, key_parts, value_parts = ([], [], [])
    for head in range(kv_heads):
        block = query[:, head * group * HD : (head + 1) * group * HD].reshape(seg * group, HD)
        grad_block = dout[:, head * group * HD : (head + 1) * group * HD].reshape(seg * group, HD)
        key_head = cache[:, head * HD : (head + 1) * HD]
        value_head = cache[:, half + head * HD : half + (head + 1) * HD]
        scores = (jnp.dot(block, key_head.T, preferred_element_type=jnp.float32) * scale).reshape(
            seg, group, seq_len
        )
        probs = masked_softmax(scores, allowed).reshape(seg * group, seq_len)
        rounded = probs.astype(jnp.bfloat16)
        mixed = jnp.dot(rounded, value_head, preferred_element_type=jnp.float32)
        delta = jnp.sum(grad_block.astype(jnp.float32) * mixed, axis=1, keepdims=True)
        along = jnp.dot(grad_block, value_head.T, preferred_element_type=jnp.float32)
        dscore = (probs * (along - delta)).astype(jnp.bfloat16)
        query_parts.append(
            (jnp.dot(dscore, key_head, preferred_element_type=jnp.float32) * scale).reshape(
                seg, group * HD
            )
        )
        dscore_own = lax.dynamic_slice_in_dim(dscore, start, seg, 1)
        rounded_own = lax.dynamic_slice_in_dim(rounded, start, seg, 1)
        key_parts.append(jnp.dot(dscore_own.T, block, preferred_element_type=jnp.float32) * scale)
        value_parts.append(jnp.dot(rounded_own.T, grad_block, preferred_element_type=jnp.float32))
    grad_query = jnp.concatenate(query_parts, axis=1).astype(jnp.bfloat16)
    kv_grad = jnp.concatenate(key_parts + value_parts, axis=1)
    kv_grad = jnp.where(live, kv_grad, 0.0).astype(jnp.bfloat16)
    return (grad_query, kv_grad)


def shards(fwd_x, fwd_q, bwd_x, bwd_q, bwd_dout, cache_kv, kv_weight, seg_lengths):
    front_x = fwd_x[0, 0]
    front_q = fwd_q[0, 0]
    back_x = bwd_x[0, 0]
    back_q = bwd_q[0, 0]
    back_dout = bwd_dout[0, 0]
    cache = cache_kv[0, 0]
    shard = kv_weight[0]
    lengths = seg_lengths[0, 0]
    columns = front_x
    own_kv = jnp.dot(
        columns, lax.all_gather(shard, "dp", axis=0, tiled=True), preferred_element_type=jnp.float32
    ).astype(jnp.bfloat16)
    fwd_out = forward_segment(front_q, own_kv, cache, lengths[3])
    grad_query, kv_grad = backward_segment(back_q, back_dout, cache, lengths[2], lengths[3])
    input_grad = jnp.dot(
        kv_grad,
        lax.all_gather(shard, "dp", axis=0, tiled=True).T,
        preferred_element_type=jnp.float32,
    ).astype(jnp.bfloat16)
    columns = back_x
    weight_grad = lax.psum_scatter(
        jnp.dot(columns.T, kv_grad, preferred_element_type=jnp.float32),
        "dp",
        scatter_dimension=0,
        tiled=True,
    )
    next_act = shifted(fwd_out, "pipe", 1)
    prev_grad = shifted(input_grad, "pipe", -1)
    return (next_act[None, None], grad_query[None, None], prev_grad[None, None], weight_grad[None])

MESH = pl.DeviceIdType.MESH
LANES = 128
LOG2E = math.log2(math.e)


def dot(a, b, dims):
    return lax.dot_general(a, b, (dims, ((), ())), preferred_element_type=jnp.float32)


def heads_of(ref, g, group):
    width = group * HD
    columns = ref[:, pl.ds(pl.multiple_of(g * width, LANES), width)]
    return jnp.concatenate([columns[:, h * HD : (h + 1) * HD] for h in range(group)], axis=0)


def heads_back(value, group):
    seg = value.shape[0] // group
    return jnp.concatenate([value[h * seg : (h + 1) * seg] for h in range(group)], axis=1)


def fused(
    chips,
    stages,
    len_ref,
    fx_ref,
    fq_ref,
    bx_ref,
    bq_ref,
    bd_ref,
    cache_ref,
    w_ref,
    next_ref,
    gq_ref,
    prev_ref,
    wg_ref,
    cache,
    bq,
    bd,
    fq,
    weight,
    xf,
    xb,
    part,
    own_in,
    kvs,
    kg,
    high,
    fout,
    gq,
    igrad,
    terms,
    other,
    load_sem,
    xf_s,
    xf_r,
    xb_s,
    xb_r,
    own_s,
    own_r,
    kg_s,
    kg_r,
    ig_s,
    ig_r,
    na_s,
    na_r,
    pair_s,
    pair_r,
    out_sem,
):
    seg, model = bq.shape
    seq_len, both = cache.shape
    half = both // 2
    kv_heads = half // HD
    group = model // half
    window = model // chips
    shard = w_ref.shape[0]
    width = group * HD
    low = seq_len - 2 * seg
    scale = 1.0 / math.sqrt(HD)
    me = lax.axis_index("dp")
    stage = lax.axis_index("pipe")
    chip, core = me // 2, me % 2
    has_next, has_prev = stage < stages - 1, stage > 0

    def at_chip(k):
        return ((chip + k) % chips) * 2 + core

    def columns_of(index):
        return pl.ds(pl.multiple_of(index * window, LANES), window)

    loads = [
        pltpu.make_async_copy(source, target, load_sem.at[i])
        for i, (source, target) in enumerate(
            [
                (bq_ref, bq),
                (cache_ref, cache),
                (bd_ref, bd),
                (fx_ref.at[:, columns_of(chip)], xf.at[0]),
                (w_ref, weight.at[pl.ds(pl.multiple_of(core * shard, 64), shard)]),
                (fq_ref, fq),
                (bx_ref.at[:, columns_of(chip)], xb.at[0]),
            ]
        )
    ]
    for load in loads:
        load.start()

    barrier = pltpu.get_barrier_semaphore()
    sibling = chip * 2 + 1 - core
    pl.semaphore_signal(barrier, inc=1, device_id={"dp": sibling}, device_id_type=MESH)
    for k in range(1, chips):
        pl.semaphore_signal(barrier, inc=1, device_id={"dp": at_chip(k)}, device_id_type=MESH)

    @pl.when(has_next)
    def _():
        for k in range(chips):
            pl.semaphore_signal(
                barrier, inc=1, device_id={"dp": at_chip(k), "pipe": stage + 1}, device_id_type=MESH
            )

    @pl.when(has_prev)
    def _():
        for k in range(chips):
            pl.semaphore_signal(
                barrier, inc=1, device_id={"dp": at_chip(k), "pipe": stage - 1}, device_id_type=MESH
            )

    sides = (stage + stages - 1) // stages + (2 * stages - 2 - stage) // stages
    pl.semaphore_wait(barrier, chips * (1 + sides))

    def remote(source, target, send, recv, device):
        return pltpu.make_async_remote_copy(
            src_ref=source,
            dst_ref=target,
            send_sem=send,
            recv_sem=recv,
            device_id=device,
            device_id_type=MESH,
        )

    def columns_copy(x_ref, slots, send, recv, k):
        there = (chip + k) % chips
        return remote(
            x_ref.at[:, columns_of(there)], slots.at[k], send.at[k], recv.at[k], {"dp": at_chip(k)}
        )

    xf_copies = [columns_copy(fx_ref, xf, xf_s, xf_r, k) for k in range(1, chips)]
    xb_copies = [columns_copy(bx_ref, xb, xb_s, xb_r, k) for k in range(1, chips)]
    w_copy = remote(
        w_ref,
        weight.at[pl.ds(pl.multiple_of(core * shard, 64), shard)],
        pair_s.at[0],
        pair_r.at[0],
        {"dp": sibling},
    )
    own_copies = [
        remote(part.at[k], own_in.at[k], own_s.at[k], own_r.at[k], {"dp": at_chip(chips - k)})
        for k in range(1, chips)
    ]
    kg_copies = [
        remote(kg.at[0], kg.at[k], kg_s.at[k], kg_r.at[k], {"dp": at_chip(k)})
        for k in range(1, chips)
    ]
    ig_copies = [
        remote(
            igrad.at[k],
            prev_ref.at[:, columns_of(chip)],
            ig_s.at[k],
            ig_r.at[k],
            {"dp": at_chip(chips - k), "pipe": stage - 1},
        )
        for k in range(chips)
    ]

    def next_copy(g):
        piece = pl.ds(pl.multiple_of(g * width, LANES), width)
        return remote(
            fout.at[:, piece],
            next_ref.at[:, piece],
            na_s.at[g],
            na_r.at[g],
            {"dp": me, "pipe": stage + 1},
        )

    for copy in xf_copies:
        copy.start()
    w_copy.start()
    for copy in xb_copies:
        copy.start()

    third, fourth = len_ref[0, 0, 2], len_ref[0, 0, 3]
    start3 = seq_len - fourth
    start2 = start3 - third
    row = lax.broadcasted_iota(jnp.int32, (seg, 1), 0)
    live2 = jnp.where(row < third, 1.0, 0.0)
    live3 = jnp.where(row < fourth, 1.0, 0.0)
    column = lax.broadcasted_iota(jnp.int32, (seg, seq_len - low), 1) + low
    row_wide = lax.broadcasted_iota(jnp.int32, (seg, seq_len - low), 0)

    def bias(start):
        piece = jnp.where(column <= start + row_wide, 0.0, -1e30)
        return jnp.concatenate([piece] * group, axis=0)

    def softmax_parts(scores_low, scores_high, start):
        scores_high = scores_high + bias(start)
        top = jnp.maximum(
            jnp.max(scores_low, axis=1, keepdims=True), jnp.max(scores_high, axis=1, keepdims=True)
        )
        raised_low = jnp.exp2((scores_low - top) * (scale * LOG2E))
        raised_high = jnp.exp2((scores_high - top) * (scale * LOG2E))
        total = jnp.sum(raised_low, axis=1, keepdims=True) + jnp.sum(
            raised_high, axis=1, keepdims=True
        )
        return raised_low, raised_high, 1.0 / total

    def lanes(start):
        return pl.ds(pl.multiple_of(start, LANES), HD)

    def project():
        loads[3].wait()
        loads[4].wait()
        w_copy.wait()
        for copy in xf_copies:
            copy.wait()
        product = dot(xf[...].reshape(chips * seg, window), weight[...], ((1,), (0,)))
        part[...] = product.astype(jnp.bfloat16).reshape(part.shape)
        for copy in own_copies:
            copy.start()

    loads[0].wait()
    loads[1].wait()
    loads[2].wait()

    @pl.loop(0, kv_heads)
    def _(g):
        @pl.when(g == kv_heads // 2)
        def _():
            project()

        query = heads_of(bq, g, group)
        dout = heads_of(bd, g, group).astype(jnp.float32)
        dout = (dout * jnp.concatenate([live2] * group, axis=0)).astype(jnp.bfloat16)
        keys = cache[:, lanes(g * HD)]
        values = cache[:, lanes(half + g * HD)]
        scores = dot(query, keys, ((1,), (1,)))
        e_low, e_high, inverse = softmax_parts(scores[:, :low], scores[:, low:], start2)
        probs = jnp.concatenate([e_low, e_high], axis=1) * inverse
        rounded = probs.astype(jnp.bfloat16)
        mixed = dot(rounded, values, ((1,), (0,)))
        delta = jnp.sum(dout.astype(jnp.float32) * mixed, axis=1, keepdims=True)
        along = dot(dout, values, ((1,), (1,)))
        dscore = (probs * (along - delta)).astype(jnp.bfloat16)
        grad = dot(dscore, keys, ((1,), (0,))) * scale
        gq[:, pl.ds(pl.multiple_of(g * width, LANES), width)] = heads_back(grad, group).astype(
            jnp.bfloat16
        )
        key_grad = dot(dscore[:, low:], query, ((0,), (0,))) * scale
        value_grad = dot(rounded[:, low:], dout, ((0,), (0,)))
        kvs[:, lanes(g * HD)] = key_grad.astype(jnp.bfloat16)
        kvs[:, lanes(half + g * HD)] = value_grad.astype(jnp.bfloat16)

    pick = (column == start2 + row_wide) & (row_wide < third)
    pick = jnp.where(pick, 1.0, 0.0).astype(jnp.bfloat16)
    kg[0] = dot(pick, kvs[...], ((1,), (0,))).astype(jnp.bfloat16)
    for copy in kg_copies:
        copy.start()
    gq_out = pltpu.make_async_copy(gq, gq_ref, out_sem.at[0])
    gq_out.start()

    for copy in own_copies:
        copy.wait()
    own = part[0].astype(jnp.float32)
    for k in range(1, chips):
        own = own + own_in[k].astype(jnp.float32)
    own = own.astype(jnp.bfloat16)
    spot = lax.broadcasted_iota(jnp.int32, (seq_len - low, seg), 0) + low
    source = lax.broadcasted_iota(jnp.int32, (seq_len - low, seg), 1)
    place = jnp.where(spot == start3 + source, 1.0, 0.0).astype(jnp.bfloat16)
    moved = dot(place, own, ((1,), (0,)))
    stored = lax.broadcasted_iota(jnp.int32, (seq_len - low, both), 0) + low < start3
    high[...] = jnp.where(stored, cache[low:, :].astype(jnp.float32), moved).astype(jnp.bfloat16)
    loads[5].wait()

    @pl.loop(0, kv_heads)
    def _(g):
        query = heads_of(fq, g, group)
        s_low = dot(query, cache[:low, lanes(g * HD)], ((1,), (1,)))
        s_high = dot(query, high[:, lanes(g * HD)], ((1,), (1,)))
        e_low, e_high, inverse = softmax_parts(s_low, s_high, start3)
        mixed = dot(e_low.astype(jnp.bfloat16), cache[:low, lanes(half + g * HD)], ((1,), (0,)))
        mixed = mixed + dot(
            e_high.astype(jnp.bfloat16), high[:, lanes(half + g * HD)], ((1,), (0,))
        )
        mixed = mixed * (inverse * jnp.concatenate([live3] * group, axis=0))
        fout[:, pl.ds(pl.multiple_of(g * width, LANES), width)] = heads_back(mixed, group).astype(
            jnp.bfloat16
        )

        @pl.when(has_next)
        def _():
            next_copy(g).start()

    for copy in kg_copies:
        copy.wait()
    gathered = kg[...].reshape(chips * seg, both)

    @pl.when(has_prev)
    def _():
        grad = dot(gathered, weight[...], ((1,), (1,)))
        igrad[...] = grad.astype(jnp.bfloat16).reshape(igrad.shape)
        for copy in ig_copies:
            copy.start()

    loads[6].wait()
    for copy in xb_copies:
        copy.wait()
    terms[...] = dot(xb[...].reshape(chips * seg, window), gathered, ((0,), (0,)))
    t_copy = remote(
        terms.at[pl.ds(pl.multiple_of((1 - core) * shard, 64), shard)],
        other,
        pair_s.at[1],
        pair_r.at[1],
        {"dp": sibling},
    )
    t_copy.start()

    @pl.when(jnp.logical_not(has_prev))
    def _():
        igrad[...] = jnp.zeros_like(igrad)
        fills = [
            pltpu.make_async_copy(igrad.at[k], next_ref.at[:, columns_of(k)], ig_s.at[k])
            for k in range(chips)
        ]
        for fill in fills:
            fill.start()
        for fill in fills:
            fill.wait()

    t_copy.wait()
    other[...] = other[...] + terms[pl.ds(pl.multiple_of(core * shard, 64), shard), :]
    wg_out = pltpu.make_async_copy(other, wg_ref, out_sem.at[1])
    wg_out.start()

    @pl.when(has_next)
    def _():
        for g in range(kv_heads):
            next_copy(g).wait_send()
        for k in range(chips):
            ig_copies[k].wait_recv()

    @pl.when(jnp.logical_not(has_next))
    def _():
        fout[...] = jnp.zeros_like(fout)
        fill = pltpu.make_async_copy(fout, prev_ref, out_sem.at[2])
        fill.start()
        fill.wait()

    @pl.when(has_prev)
    def _():
        for g in range(kv_heads):
            next_copy(g).wait_recv()
        for k in range(chips):
            ig_copies[k].wait_send()

    gq_out.wait()
    wg_out.wait()


def fused_shards(chips, stages, fwd_x, fwd_q, bwd_x, bwd_q, bwd_dout, cache_kv, kv_weight, lengths):
    seg, model = fwd_x.shape[2:]
    seq_len, both = cache_kv.shape[2:]
    shard = kv_weight.shape[1]
    window = model // chips
    kv_heads = both // 2 // HD
    wide = jax.ShapeDtypeStruct((seg, model), jnp.bfloat16)
    vmem, dma = pltpu.VMEM, pltpu.SemaphoreType.DMA
    bf16, f32 = jnp.bfloat16, jnp.float32
    outs = pl.pallas_call(
        functools.partial(fused, chips, stages),
        out_shape=(wide, wide, wide, jax.ShapeDtypeStruct((shard, both), f32)),
        in_specs=[pl.BlockSpec(memory_space=pltpu.SMEM)] + [pl.BlockSpec(memory_space=pl.ANY)] * 7,
        out_specs=[pl.BlockSpec(memory_space=pl.ANY)] * 4,
        scratch_shapes=[
            vmem((seq_len, both), bf16),
            vmem((seg, model), bf16),
            vmem((seg, model), bf16),
            vmem((seg, model), bf16),
            vmem((2 * shard, both), bf16),
            vmem((chips, seg, window), bf16),
            vmem((chips, seg, window), bf16),
            vmem((chips, seg, both), bf16),
            vmem((chips, seg, both), bf16),
            vmem((2 * seg, both), bf16),
            vmem((chips, seg, both), bf16),
            vmem((2 * seg, both), bf16),
            vmem((seg, model), bf16),
            vmem((seg, model), bf16),
            vmem((chips, seg, window), bf16),
            vmem((2 * shard, both), f32),
            vmem((shard, both), f32),
            dma((7,)),
        ]
        + [dma((chips,))] * 10
        + [dma((kv_heads,)), dma((kv_heads,)), dma((2,)), dma((2,)), dma((3,))],
        compiler_params=pltpu.CompilerParams(
            collective_id=0, has_side_effects=True, vmem_limit_bytes=56 * 1024 * 1024
        ),
    )(
        lengths,
        fwd_x[0, 0],
        fwd_q[0, 0],
        bwd_x[0, 0],
        bwd_q[0, 0],
        bwd_dout[0, 0],
        cache_kv[0, 0],
        kv_weight[0],
    )
    next_act, grad_query, prev_grad, weight_grad = outs
    return (next_act[None, None], grad_query[None, None], prev_grad[None, None], weight_grad[None])


def solution(mesh):
    ranks, stages = mesh.shape["dp"], mesh.shape["pipe"]

    def body(fwd_x, *rest):
        if ranks % 2 == 0 and fwd_x.shape[-1] % (ranks // 2 * LANES) == 0:
            return fused_shards(ranks // 2, stages, fwd_x, *rest)
        return shards(fwd_x, *rest)

    return jax.shard_map(
        body,
        mesh=mesh,
        in_specs=(
            P("pipe", "dp", None, None),
            P("pipe", "dp", None, None),
            P("pipe", "dp", None, None),
            P("pipe", "dp", None, None),
            P("pipe", "dp", None, None),
            P("pipe", "dp", None, None),
            P("pipe", "dp", None),
            P("pipe", "dp", None),
        ),
        out_specs=(
            P("pipe", "dp", None, None),
            P("pipe", "dp", None, None),
            P("pipe", "dp", None, None),
            P("pipe", "dp", None),
        ),
        check_vma=False,
    )
```

```python
import functools
import math

import jax
import jax.numpy as jnp
from jax import lax
from jax.experimental import pallas as pl
from jax.experimental.pallas import tpu as pltpu
from jax.sharding import PartitionSpec as P

HD = 128


def shifted(value, axis, steps):
    count = lax.axis_size(axis)
    first, last = (max(0, -steps), min(count, count - steps))
    return lax.ppermute(value, axis, [(source, source + steps) for source in range(first, last)])


def masked_softmax(scores, allowed):
    masked = jnp.where(allowed[:, None, :], scores, -1e30)
    top = jnp.max(masked, axis=-1, keepdims=True)
    raised = jnp.exp(masked - top)
    return raised / jnp.sum(raised, axis=-1, keepdims=True)


def forward_segment(query, own_kv, cache, length):
    seg = query.shape[0]
    seq_len = cache.shape[0]
    half = cache.shape[1] // 2
    kv_heads = half // HD
    group = query.shape[1] // half
    scale = 1.0 / math.sqrt(HD)
    start = seq_len - length
    rows = jnp.arange(seg, dtype=jnp.int32)
    cache_ok = jnp.broadcast_to(
        jnp.arange(seq_len, dtype=jnp.int32)[None, :] < start, (seg, seq_len)
    )
    own_ok = (rows[None, :] <= rows[:, None]) & (rows[None, :] < length)
    allowed = jnp.concatenate([cache_ok, own_ok], axis=1)
    keys = jnp.concatenate([cache[:, :half], own_kv[:, :half]], axis=0)
    values = jnp.concatenate([cache[:, half:], own_kv[:, half:]], axis=0)
    pieces = []
    for head in range(kv_heads):
        block = query[:, head * group * HD : (head + 1) * group * HD].reshape(seg * group, HD)
        key_head = keys[:, head * HD : (head + 1) * HD]
        scores = (jnp.dot(block, key_head.T, preferred_element_type=jnp.float32) * scale).reshape(
            seg, group, -1
        )
        probs = masked_softmax(scores, allowed).astype(jnp.bfloat16).reshape(seg * group, -1)
        mixed = jnp.dot(
            probs, values[:, head * HD : (head + 1) * HD], preferred_element_type=jnp.float32
        )
        pieces.append(mixed.reshape(seg, group * HD))
    result = jnp.concatenate(pieces, axis=1)
    return jnp.where((rows < length)[:, None], result, 0.0).astype(jnp.bfloat16)


def backward_segment(query, dout, cache, third, fourth):
    seg = query.shape[0]
    seq_len = cache.shape[0]
    half = cache.shape[1] // 2
    kv_heads = half // HD
    group = query.shape[1] // half
    scale = 1.0 / math.sqrt(HD)
    start = seq_len - fourth - third
    rows = jnp.arange(seg, dtype=jnp.int32)
    allowed = jnp.arange(seq_len, dtype=jnp.int32)[None, :] <= start + rows[:, None]
    live = (rows < third)[:, None]
    dout = jnp.where(live, dout, jnp.zeros_like(dout))
    query_parts, key_parts, value_parts = ([], [], [])
    for head in range(kv_heads):
        block = query[:, head * group * HD : (head + 1) * group * HD].reshape(seg * group, HD)
        grad_block = dout[:, head * group * HD : (head + 1) * group * HD].reshape(seg * group, HD)
        key_head = cache[:, head * HD : (head + 1) * HD]
        value_head = cache[:, half + head * HD : half + (head + 1) * HD]
        scores = (jnp.dot(block, key_head.T, preferred_element_type=jnp.float32) * scale).reshape(
            seg, group, seq_len
        )
        probs = masked_softmax(scores, allowed).reshape(seg * group, seq_len)
        rounded = probs.astype(jnp.bfloat16)
        mixed = jnp.dot(rounded, value_head, preferred_element_type=jnp.float32)
        delta = jnp.sum(grad_block.astype(jnp.float32) * mixed, axis=1, keepdims=True)
        along = jnp.dot(grad_block, value_head.T, preferred_element_type=jnp.float32)
        dscore = (probs * (along - delta)).astype(jnp.bfloat16)
        query_parts.append(
            (jnp.dot(dscore, key_head, preferred_element_type=jnp.float32) * scale).reshape(
                seg, group * HD
            )
        )
        dscore_own = lax.dynamic_slice_in_dim(dscore, start, seg, 1)
        rounded_own = lax.dynamic_slice_in_dim(rounded, start, seg, 1)
        key_parts.append(jnp.dot(dscore_own.T, block, preferred_element_type=jnp.float32) * scale)
        value_parts.append(jnp.dot(rounded_own.T, grad_block, preferred_element_type=jnp.float32))
    grad_query = jnp.concatenate(query_parts, axis=1).astype(jnp.bfloat16)
    kv_grad = jnp.concatenate(key_parts + value_parts, axis=1)
    kv_grad = jnp.where(live, kv_grad, 0.0).astype(jnp.bfloat16)
    return (grad_query, kv_grad)


def shards(fwd_x, fwd_q, bwd_x, bwd_q, bwd_dout, cache_kv, kv_weight, seg_lengths):
    front_x = fwd_x[0, 0]
    front_q = fwd_q[0, 0]
    back_x = bwd_x[0, 0]
    back_q = bwd_q[0, 0]
    back_dout = bwd_dout[0, 0]
    cache = cache_kv[0, 0]
    shard = kv_weight[0]
    lengths = seg_lengths[0, 0]
    columns = front_x
    own_kv = jnp.dot(
        columns, lax.all_gather(shard, "dp", axis=0, tiled=True), preferred_element_type=jnp.float32
    ).astype(jnp.bfloat16)
    fwd_out = forward_segment(front_q, own_kv, cache, lengths[3])
    grad_query, kv_grad = backward_segment(back_q, back_dout, cache, lengths[2], lengths[3])
    input_grad = jnp.dot(
        kv_grad,
        lax.all_gather(shard, "dp", axis=0, tiled=True).T,
        preferred_element_type=jnp.float32,
    ).astype(jnp.bfloat16)
    columns = back_x
    weight_grad = lax.psum_scatter(
        jnp.dot(columns.T, kv_grad, preferred_element_type=jnp.float32),
        "dp",
        scatter_dimension=0,
        tiled=True,
    )
    next_act = shifted(fwd_out, "pipe", 1)
    prev_grad = shifted(input_grad, "pipe", -1)
    return (next_act[None, None], grad_query[None, None], prev_grad[None, None], weight_grad[None])

MESH = pl.DeviceIdType.MESH
LANES = 128
LOG2E = math.log2(math.e)


def dot(a, b, dims):
    return lax.dot_general(a, b, (dims, ((), ())), preferred_element_type=jnp.float32)


def heads_of(ref, g, group):
    width = group * HD
    columns = ref[:, pl.ds(pl.multiple_of(g * width, LANES), width)]
    return jnp.concatenate([columns[:, h * HD : (h + 1) * HD] for h in range(group)], axis=0)


def heads_back(value, group):
    seg = value.shape[0] // group
    return jnp.concatenate([value[h * seg : (h + 1) * seg] for h in range(group)], axis=1)


def fused(
    chips,
    stages,
    len_ref,
    fx_ref,
    fq_ref,
    bx_ref,
    bq_ref,
    bd_ref,
    cache_ref,
    w_ref,
    next_ref,
    gq_ref,
    prev_ref,
    wg_ref,
    cache,
    bq,
    bd,
    fq,
    weight,
    xf,
    xb,
    part,
    own_in,
    kg,
    high,
    fout,
    gq,
    igrad,
    terms,
    other,
    load_sem,
    xf_s,
    xf_r,
    xb_s,
    xb_r,
    own_s,
    own_r,
    kg_s,
    kg_r,
    ig_s,
    ig_r,
    na_s,
    na_r,
    pair_s,
    pair_r,
    out_sem,
):
    seg, model = bq.shape
    seq_len, both = cache.shape
    half = both // 2
    kv_heads = half // HD
    group = model // half
    window = model // chips
    shard = w_ref.shape[0]
    width = group * HD
    low = seq_len - 2 * seg
    scale = 1.0 / math.sqrt(HD)
    me = lax.axis_index("dp")
    stage = lax.axis_index("pipe")
    chip, core = me // 2, me % 2
    has_next, has_prev = stage < stages - 1, stage > 0

    def at_chip(k):
        return ((chip + k) % chips) * 2 + core

    def columns_of(index):
        return pl.ds(pl.multiple_of(index * window, LANES), window)

    loads = [
        pltpu.make_async_copy(source, target, load_sem.at[i])
        for i, (source, target) in enumerate(
            [
                (bq_ref, bq),
                (cache_ref, cache),
                (bd_ref, bd),
                (fx_ref.at[:, columns_of(chip)], xf.at[0]),
                (w_ref, weight.at[pl.ds(pl.multiple_of(core * shard, 64), shard)]),
                (fq_ref, fq),
                (bx_ref.at[:, columns_of(chip)], xb.at[0]),
            ]
        )
    ]
    for load in loads:
        load.start()

    barrier = pltpu.get_barrier_semaphore()
    sibling = chip * 2 + 1 - core
    pl.semaphore_signal(barrier, inc=1, device_id={"dp": sibling}, device_id_type=MESH)
    for k in range(1, chips):
        pl.semaphore_signal(barrier, inc=1, device_id={"dp": at_chip(k)}, device_id_type=MESH)

    @pl.when(has_next)
    def _():
        for k in range(chips):
            pl.semaphore_signal(
                barrier, inc=1, device_id={"dp": at_chip(k), "pipe": stage + 1}, device_id_type=MESH
            )

    @pl.when(has_prev)
    def _():
        for k in range(chips):
            pl.semaphore_signal(
                barrier, inc=1, device_id={"dp": at_chip(k), "pipe": stage - 1}, device_id_type=MESH
            )

    sides = (stage + stages - 1) // stages + (2 * stages - 2 - stage) // stages
    pl.semaphore_wait(barrier, chips * (1 + sides))

    def remote(source, target, send, recv, device):
        return pltpu.make_async_remote_copy(
            src_ref=source,
            dst_ref=target,
            send_sem=send,
            recv_sem=recv,
            device_id=device,
            device_id_type=MESH,
        )

    def columns_copy(x_ref, slots, send, recv, k):
        there = (chip + k) % chips
        return remote(
            x_ref.at[:, columns_of(there)], slots.at[k], send.at[k], recv.at[k], {"dp": at_chip(k)}
        )

    xf_copies = [columns_copy(fx_ref, xf, xf_s, xf_r, k) for k in range(1, chips)]
    xb_copies = [columns_copy(bx_ref, xb, xb_s, xb_r, k) for k in range(1, chips)]
    w_copy = remote(
        w_ref,
        weight.at[pl.ds(pl.multiple_of(core * shard, 64), shard)],
        pair_s.at[0],
        pair_r.at[0],
        {"dp": sibling},
    )
    own_copies = [
        remote(part.at[k], own_in.at[k], own_s.at[k], own_r.at[k], {"dp": at_chip(chips - k)})
        for k in range(1, chips)
    ]
    kg_copies = [
        remote(kg.at[0], kg.at[k], kg_s.at[k], kg_r.at[k], {"dp": at_chip(k)})
        for k in range(1, chips)
    ]

    def kg_piece(k, piece):
        return remote(
            kg.at[0, :, piece], kg.at[k, :, piece], kg_s.at[k], kg_r.at[k], {"dp": at_chip(k)}
        )

    ig_copies = [
        remote(
            igrad.at[k],
            prev_ref.at[:, columns_of(chip)],
            ig_s.at[k],
            ig_r.at[k],
            {"dp": at_chip(chips - k), "pipe": stage - 1},
        )
        for k in range(chips)
    ]

    def next_copy(g):
        piece = pl.ds(pl.multiple_of(g * width, LANES), width)
        return remote(
            fout.at[:, piece],
            next_ref.at[:, piece],
            na_s.at[g],
            na_r.at[g],
            {"dp": me, "pipe": stage + 1},
        )

    for copy in xf_copies:
        copy.start()
    w_copy.start()

    third, fourth = len_ref[0, 0, 2], len_ref[0, 0, 3]
    start3 = seq_len - fourth
    start2 = start3 - third
    row = lax.broadcasted_iota(jnp.int32, (seg, 1), 0)
    live2 = jnp.where(row < third, 1.0, 0.0)
    live3 = jnp.where(row < fourth, 1.0, 0.0)
    column = lax.broadcasted_iota(jnp.int32, (seg, seq_len - low), 1) + low
    row_wide = lax.broadcasted_iota(jnp.int32, (seg, seq_len - low), 0)

    def bias(start):
        piece = jnp.where(column <= start + row_wide, 0.0, -1e30)
        return jnp.concatenate([piece] * group, axis=0)

    def softmax_parts(scores_low, scores_high, start):
        scores_high = scores_high + bias(start)
        top = jnp.maximum(
            jnp.max(scores_low, axis=1, keepdims=True), jnp.max(scores_high, axis=1, keepdims=True)
        )
        raised_low = jnp.exp2((scores_low - top) * (scale * LOG2E))
        raised_high = jnp.exp2((scores_high - top) * (scale * LOG2E))
        total = jnp.sum(raised_low, axis=1, keepdims=True) + jnp.sum(
            raised_high, axis=1, keepdims=True
        )
        return raised_low, raised_high, 1.0 / total

    def lanes(start):
        return pl.ds(pl.multiple_of(start, LANES), HD)

    def project():
        loads[3].wait()
        loads[4].wait()
        w_copy.wait()
        for copy in xf_copies:
            copy.wait()
        product = dot(xf[...].reshape(chips * seg, window), weight[...], ((1,), (0,)))
        part[...] = product.astype(jnp.bfloat16).reshape(part.shape)
        for copy in own_copies:
            copy.start()

    loads[0].wait()
    loads[1].wait()
    loads[2].wait()

    pick = (column == start2 + row_wide) & (row_wide < third)
    pick = jnp.where(pick, 1.0, 0.0).astype(jnp.bfloat16)

    @pl.loop(0, kv_heads)
    def _(g):
        @pl.when(g == 1)
        def _():
            for copy in xb_copies:
                copy.start()

        @pl.when(g == kv_heads // 2)
        def _():
            project()

        query = heads_of(bq, g, group)
        dout = heads_of(bd, g, group).astype(jnp.float32)
        dout = (dout * jnp.concatenate([live2] * group, axis=0)).astype(jnp.bfloat16)
        keys = cache[:, lanes(g * HD)]
        values = cache[:, lanes(half + g * HD)]
        scores = dot(query, keys, ((1,), (1,)))
        e_low, e_high, inverse = softmax_parts(scores[:, :low], scores[:, low:], start2)
        along = dot(dout, values, ((1,), (1,)))
        mixed = dot(e_low.astype(jnp.bfloat16), values[:low], ((1,), (0,)))
        mixed = mixed + dot(e_high.astype(jnp.bfloat16), values[low:], ((1,), (0,)))
        delta = jnp.sum(dout.astype(jnp.float32) * mixed, axis=1, keepdims=True) * inverse
        d_low = e_low * (along[:, :low] - delta)
        d_high = e_high * (along[:, low:] - delta)
        grad = dot(d_low.astype(jnp.bfloat16), keys[:low], ((1,), (0,)))
        grad = grad + dot(d_high.astype(jnp.bfloat16), keys[low:], ((1,), (0,)))
        grad = grad * (inverse * scale)
        key_grad = dot((d_high * inverse).astype(jnp.bfloat16), query, ((0,), (0,))) * scale
        value_grad = dot((e_high * inverse).astype(jnp.bfloat16), dout, ((0,), (0,)))
        for start, part_grad in ((g * HD, key_grad), (half + g * HD, value_grad)):
            kg[0, :, lanes(start)] = dot(
                pick, part_grad.astype(jnp.bfloat16), ((1,), (0,))
            ).astype(jnp.bfloat16)
        for k in range(1, chips):
            kg_piece(k, lanes(g * HD)).start()
            kg_piece(k, lanes(half + g * HD)).start()
        gq[:, pl.ds(pl.multiple_of(g * width, LANES), width)] = heads_back(grad, group).astype(
            jnp.bfloat16
        )

    gq_out = pltpu.make_async_copy(gq, gq_ref, out_sem.at[0])
    gq_out.start()

    for copy in own_copies:
        copy.wait()
    own = part[0].astype(jnp.float32)
    for k in range(1, chips):
        own = own + own_in[k].astype(jnp.float32)
    own = own.astype(jnp.bfloat16)
    spot = lax.broadcasted_iota(jnp.int32, (seq_len - low, seg), 0) + low
    source = lax.broadcasted_iota(jnp.int32, (seq_len - low, seg), 1)
    place = jnp.where(spot == start3 + source, 1.0, 0.0).astype(jnp.bfloat16)
    moved = dot(place, own, ((1,), (0,)))
    stored = lax.broadcasted_iota(jnp.int32, (seq_len - low, both), 0) + low < start3
    high[...] = jnp.where(stored, cache[low:, :].astype(jnp.float32), moved).astype(jnp.bfloat16)
    loads[5].wait()

    t_copy = remote(
        terms.at[pl.ds(pl.multiple_of((1 - core) * shard, 64), shard)],
        other,
        pair_s.at[1],
        pair_r.at[1],
        {"dp": sibling},
    )

    def gradients():
        for copy in kg_copies:
            copy.wait()
        gathered = kg[...].reshape(chips * seg, both)

        @pl.when(has_prev)
        def _():
            grad = dot(gathered, weight[...], ((1,), (1,)))
            igrad[...] = grad.astype(jnp.bfloat16).reshape(igrad.shape)
            for copy in ig_copies:
                copy.start()

        loads[6].wait()
        for copy in xb_copies:
            copy.wait()
        terms[...] = dot(xb[...].reshape(chips * seg, window), gathered, ((0,), (0,)))
        t_copy.start()

    @pl.loop(0, kv_heads)
    def _(g):
        @pl.when(g == 1)
        def _():
            gradients()

        query = heads_of(fq, g, group)
        s_low = dot(query, cache[:low, lanes(g * HD)], ((1,), (1,)))
        s_high = dot(query, high[:, lanes(g * HD)], ((1,), (1,)))
        e_low, e_high, inverse = softmax_parts(s_low, s_high, start3)
        mixed = dot(e_low.astype(jnp.bfloat16), cache[:low, lanes(half + g * HD)], ((1,), (0,)))
        mixed = mixed + dot(
            e_high.astype(jnp.bfloat16), high[:, lanes(half + g * HD)], ((1,), (0,))
        )
        mixed = mixed * (inverse * jnp.concatenate([live3] * group, axis=0))
        fout[:, pl.ds(pl.multiple_of(g * width, LANES), width)] = heads_back(mixed, group).astype(
            jnp.bfloat16
        )

        @pl.when(has_next)
        def _():
            next_copy(g).start()

    @pl.when(jnp.logical_not(has_prev))
    def _():
        igrad[...] = jnp.zeros_like(igrad)
        fills = [
            pltpu.make_async_copy(igrad.at[k], next_ref.at[:, columns_of(k)], ig_s.at[k])
            for k in range(chips)
        ]
        for fill in fills:
            fill.start()
        for fill in fills:
            fill.wait()

    t_copy.wait()
    other[...] = other[...] + terms[pl.ds(pl.multiple_of(core * shard, 64), shard), :]
    wg_out = pltpu.make_async_copy(other, wg_ref, out_sem.at[1])
    wg_out.start()

    @pl.when(has_next)
    def _():
        for g in range(kv_heads):
            next_copy(g).wait_send()
        for k in range(chips):
            ig_copies[k].wait_recv()

    @pl.when(jnp.logical_not(has_next))
    def _():
        fout[...] = jnp.zeros_like(fout)
        fill = pltpu.make_async_copy(fout, prev_ref, out_sem.at[2])
        fill.start()
        fill.wait()

    @pl.when(has_prev)
    def _():
        for g in range(kv_heads):
            next_copy(g).wait_recv()
        for k in range(chips):
            ig_copies[k].wait_send()

    gq_out.wait()
    wg_out.wait()


def hand_over(*refs):
    sources, targets, sem = refs[:4], refs[4:8], refs[8]
    copies = []
    for i in (3, 0, 1, 2):
        rows = sources[i].shape[0] // 4
        for j in range(4):
            piece = pl.ds(j * rows, rows)
            copies.append(
                pltpu.make_async_copy(sources[i].at[piece], targets[i].at[piece], sem.at[i, j])
            )
    for copy in copies:
        copy.start()
    for copy in copies:
        copy.wait()


def fused_shards(chips, stages, fwd_x, fwd_q, bwd_x, bwd_q, bwd_dout, cache_kv, kv_weight, lengths):
    seg, model = fwd_x.shape[2:]
    seq_len, both = cache_kv.shape[2:]
    shard = kv_weight.shape[1]
    window = model // chips
    kv_heads = both // 2 // HD
    wide = jax.ShapeDtypeStruct((seg, model), jnp.bfloat16)
    vmem, dma = pltpu.VMEM, pltpu.SemaphoreType.DMA
    bf16, f32 = jnp.bfloat16, jnp.float32
    outs = pl.pallas_call(
        functools.partial(fused, chips, stages),
        out_shape=(wide, wide, wide, jax.ShapeDtypeStruct((shard, both), f32)),
        in_specs=[pl.BlockSpec(memory_space=pltpu.SMEM)] + [pl.BlockSpec(memory_space=pl.ANY)] * 7,
        out_specs=[pl.BlockSpec(memory_space=pl.ANY)] * 4,
        scratch_shapes=[
            vmem((seq_len, both), bf16),
            vmem((seg, model), bf16),
            vmem((seg, model), bf16),
            vmem((seg, model), bf16),
            vmem((2 * shard, both), bf16),
            vmem((chips, seg, window), bf16),
            vmem((chips, seg, window), bf16),
            vmem((chips, seg, both), bf16),
            vmem((chips, seg, both), bf16),
            vmem((chips, seg, both), bf16),
            vmem((2 * seg, both), bf16),
            vmem((seg, model), bf16),
            vmem((seg, model), bf16),
            vmem((chips, seg, window), bf16),
            vmem((2 * shard, both), f32),
            vmem((shard, both), f32),
            dma((7,)),
        ]
        + [dma((chips,))] * 10
        + [dma((kv_heads,)), dma((kv_heads,)), dma((2,)), dma((2,)), dma((3,))],
        compiler_params=pltpu.CompilerParams(
            collective_id=0, has_side_effects=True, vmem_limit_bytes=56 * 1024 * 1024
        ),
    )(
        lengths,
        fwd_x[0, 0],
        fwd_q[0, 0],
        bwd_x[0, 0],
        bwd_q[0, 0],
        bwd_dout[0, 0],
        cache_kv[0, 0],
        kv_weight[0],
    )
    next_act, grad_query, prev_grad, weight_grad = pl.pallas_call(
        hand_over,
        out_shape=tuple(jax.ShapeDtypeStruct(out.shape, out.dtype) for out in outs),
        in_specs=[pl.BlockSpec(memory_space=pl.ANY)] * 4,
        out_specs=[pl.BlockSpec(memory_space=pl.ANY)] * 4,
        scratch_shapes=[dma((4, 4))],
        compiler_params=pltpu.CompilerParams(vmem_limit_bytes=56 * 1024 * 1024),
    )(*outs)
    return (next_act[None, None], grad_query[None, None], prev_grad[None, None], weight_grad[None])


def solution(mesh):
    ranks, stages = mesh.shape["dp"], mesh.shape["pipe"]

    def body(fwd_x, *rest):
        if ranks % 2 == 0 and fwd_x.shape[-1] % (ranks // 2 * LANES) == 0:
            return fused_shards(ranks // 2, stages, fwd_x, *rest)
        return shards(fwd_x, *rest)

    return jax.shard_map(
        body,
        mesh=mesh,
        in_specs=(
            P("pipe", "dp", None, None),
            P("pipe", "dp", None, None),
            P("pipe", "dp", None, None),
            P("pipe", "dp", None, None),
            P("pipe", "dp", None, None),
            P("pipe", "dp", None, None),
            P("pipe", "dp", None),
            P("pipe", "dp", None),
        ),
        out_specs=(
            P("pipe", "dp", None, None),
            P("pipe", "dp", None, None),
            P("pipe", "dp", None, None),
            P("pipe", "dp", None),
        ),
        check_vma=False,
    )
```

```python
import functools
import math

import jax
import jax.numpy as jnp
from jax import lax
from jax.experimental import pallas as pl
from jax.experimental.pallas import tpu as pltpu
from jax.sharding import PartitionSpec as P

HD = 128


def shifted(value, axis, steps):
    count = lax.axis_size(axis)
    first, last = (max(0, -steps), min(count, count - steps))
    return lax.ppermute(value, axis, [(source, source + steps) for source in range(first, last)])


def masked_softmax(scores, allowed):
    masked = jnp.where(allowed[:, None, :], scores, -1e30)
    top = jnp.max(masked, axis=-1, keepdims=True)
    raised = jnp.exp(masked - top)
    return raised / jnp.sum(raised, axis=-1, keepdims=True)


def forward_segment(query, own_kv, cache, length):
    seg = query.shape[0]
    seq_len = cache.shape[0]
    half = cache.shape[1] // 2
    kv_heads = half // HD
    group = query.shape[1] // half
    scale = 1.0 / math.sqrt(HD)
    start = seq_len - length
    rows = jnp.arange(seg, dtype=jnp.int32)
    cache_ok = jnp.broadcast_to(
        jnp.arange(seq_len, dtype=jnp.int32)[None, :] < start, (seg, seq_len)
    )
    own_ok = (rows[None, :] <= rows[:, None]) & (rows[None, :] < length)
    allowed = jnp.concatenate([cache_ok, own_ok], axis=1)
    keys = jnp.concatenate([cache[:, :half], own_kv[:, :half]], axis=0)
    values = jnp.concatenate([cache[:, half:], own_kv[:, half:]], axis=0)
    pieces = []
    for head in range(kv_heads):
        block = query[:, head * group * HD : (head + 1) * group * HD].reshape(seg * group, HD)
        key_head = keys[:, head * HD : (head + 1) * HD]
        scores = (jnp.dot(block, key_head.T, preferred_element_type=jnp.float32) * scale).reshape(
            seg, group, -1
        )
        probs = masked_softmax(scores, allowed).astype(jnp.bfloat16).reshape(seg * group, -1)
        mixed = jnp.dot(
            probs, values[:, head * HD : (head + 1) * HD], preferred_element_type=jnp.float32
        )
        pieces.append(mixed.reshape(seg, group * HD))
    result = jnp.concatenate(pieces, axis=1)
    return jnp.where((rows < length)[:, None], result, 0.0).astype(jnp.bfloat16)


def backward_segment(query, dout, cache, third, fourth):
    seg = query.shape[0]
    seq_len = cache.shape[0]
    half = cache.shape[1] // 2
    kv_heads = half // HD
    group = query.shape[1] // half
    scale = 1.0 / math.sqrt(HD)
    start = seq_len - fourth - third
    rows = jnp.arange(seg, dtype=jnp.int32)
    allowed = jnp.arange(seq_len, dtype=jnp.int32)[None, :] <= start + rows[:, None]
    live = (rows < third)[:, None]
    dout = jnp.where(live, dout, jnp.zeros_like(dout))
    query_parts, key_parts, value_parts = ([], [], [])
    for head in range(kv_heads):
        block = query[:, head * group * HD : (head + 1) * group * HD].reshape(seg * group, HD)
        grad_block = dout[:, head * group * HD : (head + 1) * group * HD].reshape(seg * group, HD)
        key_head = cache[:, head * HD : (head + 1) * HD]
        value_head = cache[:, half + head * HD : half + (head + 1) * HD]
        scores = (jnp.dot(block, key_head.T, preferred_element_type=jnp.float32) * scale).reshape(
            seg, group, seq_len
        )
        probs = masked_softmax(scores, allowed).reshape(seg * group, seq_len)
        rounded = probs.astype(jnp.bfloat16)
        mixed = jnp.dot(rounded, value_head, preferred_element_type=jnp.float32)
        delta = jnp.sum(grad_block.astype(jnp.float32) * mixed, axis=1, keepdims=True)
        along = jnp.dot(grad_block, value_head.T, preferred_element_type=jnp.float32)
        dscore = (probs * (along - delta)).astype(jnp.bfloat16)
        query_parts.append(
            (jnp.dot(dscore, key_head, preferred_element_type=jnp.float32) * scale).reshape(
                seg, group * HD
            )
        )
        dscore_own = lax.dynamic_slice_in_dim(dscore, start, seg, 1)
        rounded_own = lax.dynamic_slice_in_dim(rounded, start, seg, 1)
        key_parts.append(jnp.dot(dscore_own.T, block, preferred_element_type=jnp.float32) * scale)
        value_parts.append(jnp.dot(rounded_own.T, grad_block, preferred_element_type=jnp.float32))
    grad_query = jnp.concatenate(query_parts, axis=1).astype(jnp.bfloat16)
    kv_grad = jnp.concatenate(key_parts + value_parts, axis=1)
    kv_grad = jnp.where(live, kv_grad, 0.0).astype(jnp.bfloat16)
    return (grad_query, kv_grad)


def shards(fwd_x, fwd_q, bwd_x, bwd_q, bwd_dout, cache_kv, kv_weight, seg_lengths):
    front_x = fwd_x[0, 0]
    front_q = fwd_q[0, 0]
    back_x = bwd_x[0, 0]
    back_q = bwd_q[0, 0]
    back_dout = bwd_dout[0, 0]
    cache = cache_kv[0, 0]
    shard = kv_weight[0]
    lengths = seg_lengths[0, 0]
    columns = front_x
    own_kv = jnp.dot(
        columns, lax.all_gather(shard, "dp", axis=0, tiled=True), preferred_element_type=jnp.float32
    ).astype(jnp.bfloat16)
    fwd_out = forward_segment(front_q, own_kv, cache, lengths[3])
    grad_query, kv_grad = backward_segment(back_q, back_dout, cache, lengths[2], lengths[3])
    input_grad = jnp.dot(
        kv_grad,
        lax.all_gather(shard, "dp", axis=0, tiled=True).T,
        preferred_element_type=jnp.float32,
    ).astype(jnp.bfloat16)
    columns = back_x
    weight_grad = lax.psum_scatter(
        jnp.dot(columns.T, kv_grad, preferred_element_type=jnp.float32),
        "dp",
        scatter_dimension=0,
        tiled=True,
    )
    next_act = shifted(fwd_out, "pipe", 1)
    prev_grad = shifted(input_grad, "pipe", -1)
    return (next_act[None, None], grad_query[None, None], prev_grad[None, None], weight_grad[None])

MESH = pl.DeviceIdType.MESH
LANES = 128
LOG2E = math.log2(math.e)


def dot(a, b, dims):
    return lax.dot_general(a, b, (dims, ((), ())), preferred_element_type=jnp.float32)


def heads_of(ref, g, group):
    width = group * HD
    columns = ref[:, pl.ds(pl.multiple_of(g * width, LANES), width)]
    return jnp.concatenate([columns[:, h * HD : (h + 1) * HD] for h in range(group)], axis=0)


def heads_back(value, group):
    seg = value.shape[0] // group
    return jnp.concatenate([value[h * seg : (h + 1) * seg] for h in range(group)], axis=1)


def fused(
    chips,
    stages,
    len_ref,
    fx_ref,
    fq_ref,
    bx_ref,
    bq_ref,
    bd_ref,
    cache_ref,
    w_ref,
    next_ref,
    gq_ref,
    prev_ref,
    wg_ref,
    cache,
    bq,
    bd,
    fq,
    weight,
    xf,
    xb,
    part,
    own_in,
    kg,
    high,
    fout,
    igrad,
    terms,
    load_sem,
    xf_s,
    xf_r,
    xb_s,
    xb_r,
    own_s,
    own_r,
    kg_s,
    kg_r,
    ig_s,
    ig_r,
    na_s,
    na_r,
    pair_s,
    pair_r,
):
    seg, model = bq.shape
    seq_len, both = cache.shape
    half = both // 2
    kv_heads = half // HD
    group = model // half
    window = model // chips
    shard = w_ref.shape[0]
    width = group * HD
    low = seq_len - 2 * seg
    scale = 1.0 / math.sqrt(HD)
    me = lax.axis_index("dp")
    stage = lax.axis_index("pipe")
    chip, core = me // 2, me % 2
    has_next, has_prev = stage < stages - 1, stage > 0

    def at_chip(k):
        return ((chip + k) % chips) * 2 + core

    def columns_of(index):
        return pl.ds(pl.multiple_of(index * window, LANES), window)

    loads = [
        pltpu.make_async_copy(source, target, load_sem.at[i])
        for i, (source, target) in enumerate(
            [
                (bq_ref, bq),
                (cache_ref, cache),
                (bd_ref, bd),
                (fx_ref.at[:, columns_of(chip)], xf.at[0]),
                (w_ref, weight.at[pl.ds(pl.multiple_of(core * shard, 64), shard)]),
                (fq_ref, fq),
                (bx_ref.at[:, columns_of(chip)], xb.at[0]),
            ]
        )
    ]
    for load in loads:
        load.start()

    barrier = pltpu.get_barrier_semaphore()
    sibling = chip * 2 + 1 - core
    pl.semaphore_signal(barrier, inc=1, device_id={"dp": sibling}, device_id_type=MESH)
    for k in range(1, chips):
        pl.semaphore_signal(barrier, inc=1, device_id={"dp": at_chip(k)}, device_id_type=MESH)

    @pl.when(has_next)
    def _():
        for k in range(chips):
            pl.semaphore_signal(
                barrier, inc=1, device_id={"dp": at_chip(k), "pipe": stage + 1}, device_id_type=MESH
            )

    @pl.when(has_prev)
    def _():
        for k in range(chips):
            pl.semaphore_signal(
                barrier, inc=1, device_id={"dp": at_chip(k), "pipe": stage - 1}, device_id_type=MESH
            )

    sides = (stage + stages - 1) // stages + (2 * stages - 2 - stage) // stages
    pl.semaphore_wait(barrier, chips * (1 + sides))

    def remote(source, target, send, recv, device):
        return pltpu.make_async_remote_copy(
            src_ref=source,
            dst_ref=target,
            send_sem=send,
            recv_sem=recv,
            device_id=device,
            device_id_type=MESH,
        )

    def columns_copy(x_ref, slots, send, recv, k):
        there = (chip + k) % chips
        return remote(
            x_ref.at[:, columns_of(there)], slots.at[k], send.at[k], recv.at[k], {"dp": at_chip(k)}
        )

    xf_copies = [columns_copy(fx_ref, xf, xf_s, xf_r, k) for k in range(1, chips)]
    xb_copies = [columns_copy(bx_ref, xb, xb_s, xb_r, k) for k in range(1, chips)]
    w_copy = remote(
        w_ref,
        weight.at[pl.ds(pl.multiple_of(core * shard, 64), shard)],
        pair_s.at[0],
        pair_r.at[0],
        {"dp": sibling},
    )
    own_copies = [
        remote(part.at[k], own_in.at[k], own_s.at[k], own_r.at[k], {"dp": at_chip(chips - k)})
        for k in range(1, chips)
    ]
    kg_copies = [
        remote(kg.at[0], kg.at[k], kg_s.at[k], kg_r.at[k], {"dp": at_chip(k)})
        for k in range(1, chips)
    ]

    def kg_piece(k, piece):
        return remote(
            kg.at[0, :, piece], kg.at[k, :, piece], kg_s.at[k], kg_r.at[k], {"dp": at_chip(k)}
        )

    ig_copies = [
        remote(
            igrad.at[k],
            prev_ref.at[:, columns_of(chip)],
            ig_s.at[k],
            ig_r.at[k],
            {"dp": at_chip(chips - k), "pipe": stage - 1},
        )
        for k in range(chips)
    ]

    def next_copy(g):
        piece = pl.ds(pl.multiple_of(g * width, LANES), width)
        return remote(
            fout.at[:, piece],
            next_ref.at[:, piece],
            na_s.at[g],
            na_r.at[g],
            {"dp": me, "pipe": stage + 1},
        )

    for copy in xf_copies:
        copy.start()
    w_copy.start()

    third, fourth = len_ref[0, 0, 2], len_ref[0, 0, 3]
    start3 = seq_len - fourth
    start2 = start3 - third
    row = lax.broadcasted_iota(jnp.int32, (seg, 1), 0)
    live2 = jnp.where(row < third, 1.0, 0.0)
    live3 = jnp.where(row < fourth, 1.0, 0.0)
    column = lax.broadcasted_iota(jnp.int32, (seg, seq_len - low), 1) + low
    row_wide = lax.broadcasted_iota(jnp.int32, (seg, seq_len - low), 0)

    def bias(start):
        piece = jnp.where(column <= start + row_wide, 0.0, -1e30)
        return jnp.concatenate([piece] * group, axis=0)

    def softmax_parts(scores_low, scores_high, start):
        scores_high = scores_high + bias(start)
        top = jnp.maximum(
            jnp.max(scores_low, axis=1, keepdims=True), jnp.max(scores_high, axis=1, keepdims=True)
        )
        raised_low = jnp.exp2((scores_low - top) * (scale * LOG2E))
        raised_high = jnp.exp2((scores_high - top) * (scale * LOG2E))
        total = jnp.sum(raised_low, axis=1, keepdims=True) + jnp.sum(
            raised_high, axis=1, keepdims=True
        )
        return raised_low, raised_high, 1.0 / total

    def lanes(start):
        return pl.ds(pl.multiple_of(start, LANES), HD)

    def project():
        loads[3].wait()
        loads[4].wait()
        w_copy.wait()
        for copy in xf_copies:
            copy.wait()
        product = dot(xf[...].reshape(chips * seg, window), weight[...], ((1,), (0,)))
        part[...] = product.astype(jnp.bfloat16).reshape(part.shape)
        for copy in own_copies:
            copy.start()

    loads[0].wait()
    loads[1].wait()
    loads[2].wait()

    pick = (column == start2 + row_wide) & (row_wide < third)
    pick = jnp.where(pick, 1.0, 0.0).astype(jnp.bfloat16)

    @pl.loop(0, kv_heads)
    def _(g):
        @pl.when(g == kv_heads // 2)
        def _():
            project()

        query = heads_of(bq, g, group)
        dout = heads_of(bd, g, group).astype(jnp.float32)
        dout = (dout * jnp.concatenate([live2] * group, axis=0)).astype(jnp.bfloat16)
        keys = cache[:, lanes(g * HD)]
        values = cache[:, lanes(half + g * HD)]
        scores = dot(query, keys, ((1,), (1,)))
        e_low, e_high, inverse = softmax_parts(scores[:, :low], scores[:, low:], start2)
        along = dot(dout, values, ((1,), (1,)))
        delta = jnp.sum(e_low * along[:, :low], axis=1, keepdims=True)
        delta = delta + jnp.sum(e_high * along[:, low:], axis=1, keepdims=True)
        delta = delta * inverse
        d_low = e_low * (along[:, :low] - delta)
        d_high = e_high * (along[:, low:] - delta)
        grad = dot(d_low.astype(jnp.bfloat16), keys[:low], ((1,), (0,)))
        grad = grad + dot(d_high.astype(jnp.bfloat16), keys[low:], ((1,), (0,)))
        grad = grad * (inverse * scale)
        key_grad = dot((d_high * inverse).astype(jnp.bfloat16), query, ((0,), (0,))) * scale
        value_grad = dot((e_high * inverse).astype(jnp.bfloat16), dout, ((0,), (0,)))
        for start, part_grad in ((g * HD, key_grad), (half + g * HD, value_grad)):
            kg[0, :, lanes(start)] = dot(
                pick, part_grad.astype(jnp.bfloat16), ((1,), (0,))
            ).astype(jnp.bfloat16)
        for k in range(1, chips):
            kg_piece(k, lanes(g * HD)).start()
            kg_piece(k, lanes(half + g * HD)).start()
        gq_ref[:, pl.ds(pl.multiple_of(g * width, LANES), width)] = heads_back(grad, group).astype(
            jnp.bfloat16
        )

    for copy in xb_copies:
        copy.start()

    for copy in own_copies:
        copy.wait()
    own = part[0].astype(jnp.float32)
    for k in range(1, chips):
        own = own + own_in[k].astype(jnp.float32)
    own = own.astype(jnp.bfloat16)
    spot = lax.broadcasted_iota(jnp.int32, (seq_len - low, seg), 0) + low
    source = lax.broadcasted_iota(jnp.int32, (seq_len - low, seg), 1)
    place = jnp.where(spot == start3 + source, 1.0, 0.0).astype(jnp.bfloat16)
    moved = dot(place, own, ((1,), (0,)))
    stored = lax.broadcasted_iota(jnp.int32, (seq_len - low, both), 0) + low < start3
    high[...] = jnp.where(stored, cache[low:, :].astype(jnp.float32), moved).astype(jnp.bfloat16)
    loads[5].wait()

    t_copy = remote(
        terms.at[pl.ds(pl.multiple_of((1 - core) * shard, 64), shard)],
        wg_ref,
        pair_s.at[1],
        pair_r.at[1],
        {"dp": sibling},
    )

    def gradients():
        for copy in kg_copies:
            copy.wait()
        gathered = kg[...].reshape(chips * seg, both)

        @pl.when(has_prev)
        def _():
            grad = dot(gathered, weight[...], ((1,), (1,)))
            igrad[...] = grad.astype(jnp.bfloat16).reshape(igrad.shape)
            for copy in ig_copies:
                copy.start()

    def weight_terms():
        loads[6].wait()
        for copy in xb_copies:
            copy.wait()
        gathered = kg[...].reshape(chips * seg, both)
        terms[...] = dot(xb[...].reshape(chips * seg, window), gathered, ((0,), (0,)))
        t_copy.start()

    @pl.loop(0, kv_heads)
    def _(g):
        @pl.when(g == 1)
        def _():
            gradients()

        @pl.when(g == 2)
        def _():
            weight_terms()

        query = heads_of(fq, g, group)
        s_low = dot(query, cache[:low, lanes(g * HD)], ((1,), (1,)))
        s_high = dot(query, high[:, lanes(g * HD)], ((1,), (1,)))
        e_low, e_high, inverse = softmax_parts(s_low, s_high, start3)
        mixed = dot(e_low.astype(jnp.bfloat16), cache[:low, lanes(half + g * HD)], ((1,), (0,)))
        mixed = mixed + dot(
            e_high.astype(jnp.bfloat16), high[:, lanes(half + g * HD)], ((1,), (0,))
        )
        mixed = mixed * (inverse * jnp.concatenate([live3] * group, axis=0))
        fout[:, pl.ds(pl.multiple_of(g * width, LANES), width)] = heads_back(mixed, group).astype(
            jnp.bfloat16
        )

        @pl.when(has_next)
        def _():
            next_copy(g).start()

    @pl.when(jnp.logical_not(has_prev))
    def _():
        next_ref[...] = jnp.zeros_like(next_ref)

    @pl.when(jnp.logical_not(has_next))
    def _():
        prev_ref[...] = jnp.zeros_like(prev_ref)

    t_copy.wait()
    wg_ref[...] = wg_ref[...] + terms[pl.ds(pl.multiple_of(core * shard, 64), shard), :]

    @pl.when(has_next)
    def _():
        for g in range(kv_heads):
            next_copy(g).wait_send()
        for k in range(chips):
            ig_copies[k].wait_recv()

    @pl.when(has_prev)
    def _():
        for g in range(kv_heads):
            next_copy(g).wait_recv()
        for k in range(chips):
            ig_copies[k].wait_send()


def hand_over(*refs):
    sources, targets, sem = refs[:4], refs[4:8], refs[8]
    copies = [
        pltpu.make_async_copy(source, target, sem.at[i])
        for i, (source, target) in enumerate(zip(sources, targets))
    ]
    for copy in copies:
        copy.start()
    for copy in copies:
        copy.wait()


def fused_shards(chips, stages, fwd_x, fwd_q, bwd_x, bwd_q, bwd_dout, cache_kv, kv_weight, lengths):
    seg, model = fwd_x.shape[2:]
    seq_len, both = cache_kv.shape[2:]
    shard = kv_weight.shape[1]
    window = model // chips
    kv_heads = both // 2 // HD
    wide = pltpu.VMEM((seg, model), jnp.bfloat16)
    vmem, dma = pltpu.VMEM, pltpu.SemaphoreType.DMA
    bf16, f32 = jnp.bfloat16, jnp.float32
    outs = pl.pallas_call(
        functools.partial(fused, chips, stages),
        out_shape=(wide, wide, wide, pltpu.VMEM((shard, both), f32)),
        in_specs=[pl.BlockSpec(memory_space=pltpu.SMEM)] + [pl.BlockSpec(memory_space=pl.ANY)] * 7,
        out_specs=[pl.BlockSpec(memory_space=pltpu.VMEM)] * 4,
        scratch_shapes=[
            vmem((seq_len, both), bf16),
            vmem((seg, model), bf16),
            vmem((seg, model), bf16),
            vmem((seg, model), bf16),
            vmem((2 * shard, both), bf16),
            vmem((chips, seg, window), bf16),
            vmem((chips, seg, window), bf16),
            vmem((chips, seg, both), bf16),
            vmem((chips, seg, both), bf16),
            vmem((chips, seg, both), bf16),
            vmem((2 * seg, both), bf16),
            vmem((seg, model), bf16),
            vmem((chips, seg, window), bf16),
            vmem((2 * shard, both), f32),
            dma((7,)),
        ]
        + [dma((chips,))] * 10
        + [dma((kv_heads,)), dma((kv_heads,)), dma((2,)), dma((2,))],
        compiler_params=pltpu.CompilerParams(
            collective_id=0, has_side_effects=True, vmem_limit_bytes=59 * 1024 * 1024
        ),
    )(
        lengths,
        fwd_x[0, 0],
        fwd_q[0, 0],
        bwd_x[0, 0],
        bwd_q[0, 0],
        bwd_dout[0, 0],
        cache_kv[0, 0],
        kv_weight[0],
    )
    next_act, grad_query, prev_grad, weight_grad = pl.pallas_call(
        hand_over,
        out_shape=tuple(jax.ShapeDtypeStruct(out.shape, out.dtype) for out in outs),
        in_specs=[pl.BlockSpec(memory_space=pltpu.VMEM)] * 4,
        out_specs=[pl.BlockSpec(memory_space=pl.ANY)] * 4,
        scratch_shapes=[dma((4,))],
        compiler_params=pltpu.CompilerParams(vmem_limit_bytes=16 * 1024 * 1024),
    )(*outs)
    return (next_act[None, None], grad_query[None, None], prev_grad[None, None], weight_grad[None])


def solution(mesh):
    ranks, stages = mesh.shape["dp"], mesh.shape["pipe"]

    def body(fwd_x, *rest):
        if ranks % 2 == 0 and fwd_x.shape[-1] % (ranks // 2 * LANES) == 0:
            return fused_shards(ranks // 2, stages, fwd_x, *rest)
        return shards(fwd_x, *rest)

    return jax.shard_map(
        body,
        mesh=mesh,
        in_specs=(
            P("pipe", "dp", None, None),
            P("pipe", "dp", None, None),
            P("pipe", "dp", None, None),
            P("pipe", "dp", None, None),
            P("pipe", "dp", None, None),
            P("pipe", "dp", None, None),
            P("pipe", "dp", None),
            P("pipe", "dp", None),
        ),
        out_specs=(
            P("pipe", "dp", None, None),
            P("pipe", "dp", None, None),
            P("pipe", "dp", None, None),
            P("pipe", "dp", None),
        ),
        check_vma=False,
    )
```

```python
import functools
import math

import jax
import jax.numpy as jnp
from jax import lax
from jax.experimental import pallas as pl
from jax.experimental.pallas import tpu as pltpu
from jax.sharding import PartitionSpec as P

HD = 128


def shifted(value, axis, steps):
    count = lax.axis_size(axis)
    first, last = (max(0, -steps), min(count, count - steps))
    return lax.ppermute(value, axis, [(source, source + steps) for source in range(first, last)])


def masked_softmax(scores, allowed):
    masked = jnp.where(allowed[:, None, :], scores, -1e30)
    top = jnp.max(masked, axis=-1, keepdims=True)
    raised = jnp.exp(masked - top)
    return raised / jnp.sum(raised, axis=-1, keepdims=True)


def forward_segment(query, own_kv, cache, length):
    seg = query.shape[0]
    seq_len = cache.shape[0]
    half = cache.shape[1] // 2
    kv_heads = half // HD
    group = query.shape[1] // half
    scale = 1.0 / math.sqrt(HD)
    start = seq_len - length
    rows = jnp.arange(seg, dtype=jnp.int32)
    cache_ok = jnp.broadcast_to(
        jnp.arange(seq_len, dtype=jnp.int32)[None, :] < start, (seg, seq_len)
    )
    own_ok = (rows[None, :] <= rows[:, None]) & (rows[None, :] < length)
    allowed = jnp.concatenate([cache_ok, own_ok], axis=1)
    keys = jnp.concatenate([cache[:, :half], own_kv[:, :half]], axis=0)
    values = jnp.concatenate([cache[:, half:], own_kv[:, half:]], axis=0)
    pieces = []
    for head in range(kv_heads):
        block = query[:, head * group * HD : (head + 1) * group * HD].reshape(seg * group, HD)
        key_head = keys[:, head * HD : (head + 1) * HD]
        scores = (jnp.dot(block, key_head.T, preferred_element_type=jnp.float32) * scale).reshape(
            seg, group, -1
        )
        probs = masked_softmax(scores, allowed).astype(jnp.bfloat16).reshape(seg * group, -1)
        mixed = jnp.dot(
            probs, values[:, head * HD : (head + 1) * HD], preferred_element_type=jnp.float32
        )
        pieces.append(mixed.reshape(seg, group * HD))
    result = jnp.concatenate(pieces, axis=1)
    return jnp.where((rows < length)[:, None], result, 0.0).astype(jnp.bfloat16)


def backward_segment(query, dout, cache, third, fourth):
    seg = query.shape[0]
    seq_len = cache.shape[0]
    half = cache.shape[1] // 2
    kv_heads = half // HD
    group = query.shape[1] // half
    scale = 1.0 / math.sqrt(HD)
    start = seq_len - fourth - third
    rows = jnp.arange(seg, dtype=jnp.int32)
    allowed = jnp.arange(seq_len, dtype=jnp.int32)[None, :] <= start + rows[:, None]
    live = (rows < third)[:, None]
    dout = jnp.where(live, dout, jnp.zeros_like(dout))
    query_parts, key_parts, value_parts = ([], [], [])
    for head in range(kv_heads):
        block = query[:, head * group * HD : (head + 1) * group * HD].reshape(seg * group, HD)
        grad_block = dout[:, head * group * HD : (head + 1) * group * HD].reshape(seg * group, HD)
        key_head = cache[:, head * HD : (head + 1) * HD]
        value_head = cache[:, half + head * HD : half + (head + 1) * HD]
        scores = (jnp.dot(block, key_head.T, preferred_element_type=jnp.float32) * scale).reshape(
            seg, group, seq_len
        )
        probs = masked_softmax(scores, allowed).reshape(seg * group, seq_len)
        rounded = probs.astype(jnp.bfloat16)
        mixed = jnp.dot(rounded, value_head, preferred_element_type=jnp.float32)
        delta = jnp.sum(grad_block.astype(jnp.float32) * mixed, axis=1, keepdims=True)
        along = jnp.dot(grad_block, value_head.T, preferred_element_type=jnp.float32)
        dscore = (probs * (along - delta)).astype(jnp.bfloat16)
        query_parts.append(
            (jnp.dot(dscore, key_head, preferred_element_type=jnp.float32) * scale).reshape(
                seg, group * HD
            )
        )
        dscore_own = lax.dynamic_slice_in_dim(dscore, start, seg, 1)
        rounded_own = lax.dynamic_slice_in_dim(rounded, start, seg, 1)
        key_parts.append(jnp.dot(dscore_own.T, block, preferred_element_type=jnp.float32) * scale)
        value_parts.append(jnp.dot(rounded_own.T, grad_block, preferred_element_type=jnp.float32))
    grad_query = jnp.concatenate(query_parts, axis=1).astype(jnp.bfloat16)
    kv_grad = jnp.concatenate(key_parts + value_parts, axis=1)
    kv_grad = jnp.where(live, kv_grad, 0.0).astype(jnp.bfloat16)
    return (grad_query, kv_grad)


def shards(fwd_x, fwd_q, bwd_x, bwd_q, bwd_dout, cache_kv, kv_weight, seg_lengths):
    front_x = fwd_x[0, 0]
    front_q = fwd_q[0, 0]
    back_x = bwd_x[0, 0]
    back_q = bwd_q[0, 0]
    back_dout = bwd_dout[0, 0]
    cache = cache_kv[0, 0]
    shard = kv_weight[0]
    lengths = seg_lengths[0, 0]
    columns = front_x
    own_kv = jnp.dot(
        columns, lax.all_gather(shard, "dp", axis=0, tiled=True), preferred_element_type=jnp.float32
    ).astype(jnp.bfloat16)
    fwd_out = forward_segment(front_q, own_kv, cache, lengths[3])
    grad_query, kv_grad = backward_segment(back_q, back_dout, cache, lengths[2], lengths[3])
    input_grad = jnp.dot(
        kv_grad,
        lax.all_gather(shard, "dp", axis=0, tiled=True).T,
        preferred_element_type=jnp.float32,
    ).astype(jnp.bfloat16)
    columns = back_x
    weight_grad = lax.psum_scatter(
        jnp.dot(columns.T, kv_grad, preferred_element_type=jnp.float32),
        "dp",
        scatter_dimension=0,
        tiled=True,
    )
    next_act = shifted(fwd_out, "pipe", 1)
    prev_grad = shifted(input_grad, "pipe", -1)
    return (next_act[None, None], grad_query[None, None], prev_grad[None, None], weight_grad[None])

MESH = pl.DeviceIdType.MESH
LANES = 128
LOG2E = math.log2(math.e)


def dot(a, b, dims):
    return lax.dot_general(a, b, (dims, ((), ())), preferred_element_type=jnp.float32)


def heads_of(ref, g, group):
    width = group * HD
    columns = ref[:, pl.ds(g * width, width)]
    return jnp.concatenate([columns[:, h * HD : (h + 1) * HD] for h in range(group)], axis=0)


def heads_back(value, group):
    seg = value.shape[0] // group
    return jnp.concatenate([value[h * seg : (h + 1) * seg] for h in range(group)], axis=1)


def fused(
    chips,
    stages,
    len_ref,
    fx_ref,
    fq_ref,
    bx_ref,
    bq_ref,
    bd_ref,
    cache_ref,
    w_ref,
    next_ref,
    gq_ref,
    prev_ref,
    wg_ref,
    cache,
    bq,
    bd,
    fq,
    weight,
    xf,
    xb,
    part,
    own_in,
    kg,
    high,
    fout,
    igrad,
    terms,
    load_sem,
    xf_s,
    xf_r,
    xb_s,
    xb_r,
    own_s,
    own_r,
    kg_s,
    kg_r,
    ig_s,
    ig_r,
    na_s,
    na_r,
    pair_s,
    pair_r,
):
    seg, model = bq.shape
    seq_len, both = cache.shape
    half = both // 2
    kv_heads = half // HD
    group = model // half
    window = model // chips
    shard = w_ref.shape[0]
    width = group * HD
    low = seq_len - 2 * seg
    scale = 1.0 / math.sqrt(HD)
    me = lax.axis_index("dp")
    stage = lax.axis_index("pipe")
    chip, core = me // 2, me % 2
    has_next, has_prev = stage < stages - 1, stage > 0

    def at_chip(k):
        return ((chip + k) % chips) * 2 + core

    def columns_of(index):
        return pl.ds(pl.multiple_of(index * window, LANES), window)

    loads = [
        pltpu.make_async_copy(source, target, load_sem.at[i])
        for i, (source, target) in enumerate(
            [
                (bq_ref, bq),
                (cache_ref, cache),
                (bd_ref, bd),
                (fx_ref.at[:, columns_of(chip)], xf.at[0]),
                (w_ref, weight.at[pl.ds(pl.multiple_of(core * shard, 64), shard)]),
                (fq_ref, fq),
                (bx_ref.at[:, columns_of(chip)], xb.at[0]),
            ]
        )
    ]
    for load in loads:
        load.start()

    barrier = pltpu.get_barrier_semaphore()
    sibling = chip * 2 + 1 - core
    pl.semaphore_signal(barrier, inc=1, device_id={"dp": sibling}, device_id_type=MESH)
    for k in range(1, chips):
        pl.semaphore_signal(barrier, inc=1, device_id={"dp": at_chip(k)}, device_id_type=MESH)

    @pl.when(has_next)
    def _():
        for k in range(chips):
            pl.semaphore_signal(
                barrier, inc=1, device_id={"dp": at_chip(k), "pipe": stage + 1}, device_id_type=MESH
            )

    @pl.when(has_prev)
    def _():
        for k in range(chips):
            pl.semaphore_signal(
                barrier, inc=1, device_id={"dp": at_chip(k), "pipe": stage - 1}, device_id_type=MESH
            )

    sides = (stage + stages - 1) // stages + (2 * stages - 2 - stage) // stages
    pl.semaphore_wait(barrier, chips * (1 + sides))

    def remote(source, target, send, recv, device):
        return pltpu.make_async_remote_copy(
            src_ref=source,
            dst_ref=target,
            send_sem=send,
            recv_sem=recv,
            device_id=device,
            device_id_type=MESH,
        )

    def columns_copy(x_ref, slots, send, recv, k):
        there = (chip + k) % chips
        return remote(
            x_ref.at[:, columns_of(there)], slots.at[k], send.at[k], recv.at[k], {"dp": at_chip(k)}
        )

    xf_copies = [columns_copy(fx_ref, xf, xf_s, xf_r, k) for k in range(1, chips)]
    xb_copies = [columns_copy(bx_ref, xb, xb_s, xb_r, k) for k in range(1, chips)]
    w_copy = remote(
        w_ref,
        weight.at[pl.ds(pl.multiple_of(core * shard, 64), shard)],
        pair_s.at[0],
        pair_r.at[0],
        {"dp": sibling},
    )
    own_copies = [
        remote(part.at[k], own_in.at[k], own_s.at[k], own_r.at[k], {"dp": at_chip(chips - k)})
        for k in range(1, chips)
    ]
    kg_copies = [
        remote(kg.at[0], kg.at[k], kg_s.at[k], kg_r.at[k], {"dp": at_chip(k)})
        for k in range(1, chips)
    ]

    def kg_piece(k, piece):
        return remote(
            kg.at[0, :, piece], kg.at[k, :, piece], kg_s.at[k], kg_r.at[k], {"dp": at_chip(k)}
        )

    ig_copies = [
        remote(
            igrad.at[k],
            prev_ref.at[:, columns_of(chip)],
            ig_s.at[k],
            ig_r.at[k],
            {"dp": at_chip(chips - k), "pipe": stage - 1},
        )
        for k in range(chips)
    ]

    def next_copy(g):
        piece = pl.ds(g * width, width)
        return remote(
            fout.at[:, piece],
            next_ref.at[:, piece],
            na_s.at[g],
            na_r.at[g],
            {"dp": me, "pipe": stage + 1},
        )

    for copy in xf_copies:
        copy.start()
    w_copy.start()

    third, fourth = len_ref[0, 0, 2], len_ref[0, 0, 3]
    start3 = seq_len - fourth
    start2 = start3 - third
    row = lax.broadcasted_iota(jnp.int32, (seg, 1), 0)
    live2 = jnp.where(row < third, 1.0, 0.0)
    live3 = jnp.where(row < fourth, 1.0, 0.0)
    column = lax.broadcasted_iota(jnp.int32, (seg, seq_len - low), 1) + low
    row_wide = lax.broadcasted_iota(jnp.int32, (seg, seq_len - low), 0)

    def bias(start):
        piece = jnp.where(column <= start + row_wide, 0.0, -1e30)
        return jnp.concatenate([piece] * group, axis=0)

    def softmax_parts(scores_low, scores_high, start):
        scores_high = scores_high + bias(start)
        top = jnp.maximum(
            jnp.max(scores_low, axis=1, keepdims=True), jnp.max(scores_high, axis=1, keepdims=True)
        )
        raised_low = jnp.exp2((scores_low - top) * (scale * LOG2E))
        raised_high = jnp.exp2((scores_high - top) * (scale * LOG2E))
        total = jnp.sum(raised_low, axis=1, keepdims=True) + jnp.sum(
            raised_high, axis=1, keepdims=True
        )
        return raised_low, raised_high, 1.0 / total

    def lanes(start):
        return pl.ds(start, HD)

    def project():
        loads[3].wait()
        loads[4].wait()
        w_copy.wait()
        for copy in xf_copies:
            copy.wait()
        product = dot(xf[...].reshape(chips * seg, window), weight[...], ((1,), (0,)))
        part[...] = product.astype(jnp.bfloat16).reshape(part.shape)
        for copy in own_copies:
            copy.start()

    loads[0].wait()
    loads[1].wait()
    loads[2].wait()

    pick = (column == start2 + row_wide) & (row_wide < third)
    pick = jnp.where(pick, 1.0, 0.0).astype(jnp.bfloat16)

    def forward_begin(g):
        query = heads_of(fq, g, group)
        return query, dot(query, cache[:low, lanes(g * HD)], ((1,), (1,)))

    def forward_end(g, query, s_low):
        s_high = dot(query, high[:, lanes(g * HD)], ((1,), (1,)))
        e_low, e_high, inverse = softmax_parts(s_low, s_high, start3)
        mixed = dot(e_low.astype(jnp.bfloat16), cache[:low, lanes(half + g * HD)], ((1,), (0,)))
        mixed = mixed + dot(
            e_high.astype(jnp.bfloat16), high[:, lanes(half + g * HD)], ((1,), (0,))
        )
        mixed = mixed * (inverse * jnp.concatenate([live3] * group, axis=0))
        fout[:, pl.ds(g * width, width)] = heads_back(mixed, group).astype(jnp.bfloat16)

        @pl.when(has_next)
        def _():
            next_copy(g).start()

    def backward_begin(g):
        query = heads_of(bq, g, group)
        dout = heads_of(bd, g, group).astype(jnp.float32)
        dout = (dout * jnp.concatenate([live2] * group, axis=0)).astype(jnp.bfloat16)
        scores = dot(query, cache[:, lanes(g * HD)], ((1,), (1,)))
        along = dot(dout, cache[:, lanes(half + g * HD)], ((1,), (1,)))
        return query, dout, scores, along

    def backward_end(g, query, dout, scores, along):
        e_low, e_high, inverse = softmax_parts(scores[:, :low], scores[:, low:], start2)
        delta = jnp.sum(e_low * along[:, :low], axis=1, keepdims=True)
        delta = delta + jnp.sum(e_high * along[:, low:], axis=1, keepdims=True)
        delta = delta * inverse
        d_low = e_low * (along[:, :low] - delta)
        d_high = e_high * (along[:, low:] - delta)
        key_grad = dot((d_high * inverse).astype(jnp.bfloat16), query, ((0,), (0,))) * scale
        value_grad = dot((e_high * inverse).astype(jnp.bfloat16), dout, ((0,), (0,)))
        for start, part_grad in ((g * HD, key_grad), (half + g * HD, value_grad)):
            kg[0, :, lanes(start)] = dot(
                pick, part_grad.astype(jnp.bfloat16), ((1,), (0,))
            ).astype(jnp.bfloat16)
        for k in range(1, chips):
            kg_piece(k, lanes(g * HD)).start()
            kg_piece(k, lanes(half + g * HD)).start()
        keys = cache[:, lanes(g * HD)]
        grad = dot(d_low.astype(jnp.bfloat16), keys[:low], ((1,), (0,)))
        grad = grad + dot(d_high.astype(jnp.bfloat16), keys[low:], ((1,), (0,)))
        grad = grad * (inverse * scale)
        gq_ref[:, pl.ds(g * width, width)] = heads_back(grad, group).astype(jnp.bfloat16)

    loads[5].wait()
    state = backward_begin(0)
    for g in range(kv_heads):
        later = backward_begin(g + 1) if g + 1 < kv_heads else forward_begin(0)
        backward_end(g, *state)
        state = later
        if g == kv_heads // 2 - 1:
            project()

    for copy in xb_copies:
        copy.start()

    for copy in own_copies:
        copy.wait()
    own = part[0].astype(jnp.float32)
    for k in range(1, chips):
        own = own + own_in[k].astype(jnp.float32)
    own = own.astype(jnp.bfloat16)
    spot = lax.broadcasted_iota(jnp.int32, (seq_len - low, seg), 0) + low
    source = lax.broadcasted_iota(jnp.int32, (seq_len - low, seg), 1)
    place = jnp.where(spot == start3 + source, 1.0, 0.0).astype(jnp.bfloat16)
    moved = dot(place, own, ((1,), (0,)))
    stored = lax.broadcasted_iota(jnp.int32, (seq_len - low, both), 0) + low < start3
    high[...] = jnp.where(stored, cache[low:, :].astype(jnp.float32), moved).astype(jnp.bfloat16)

    t_copy = remote(
        terms.at[pl.ds(pl.multiple_of((1 - core) * shard, 64), shard)],
        wg_ref,
        pair_s.at[1],
        pair_r.at[1],
        {"dp": sibling},
    )

    def gradients():
        for copy in kg_copies:
            copy.wait()
        gathered = kg[...].reshape(chips * seg, both)

        @pl.when(has_prev)
        def _():
            grad = dot(gathered, weight[...], ((1,), (1,)))
            igrad[...] = grad.astype(jnp.bfloat16).reshape(igrad.shape)
            for copy in ig_copies:
                copy.start()

    def weight_terms():
        loads[6].wait()
        for copy in xb_copies:
            copy.wait()
        gathered = kg[...].reshape(chips * seg, both)
        terms[...] = dot(xb[...].reshape(chips * seg, window), gathered, ((0,), (0,)))
        t_copy.start()

    for g in range(kv_heads):
        later = forward_begin(g + 1) if g + 1 < kv_heads else None
        forward_end(g, *state)
        state = later
        if g == 0:
            gradients()
        if g == 1:
            weight_terms()

    @pl.when(jnp.logical_not(has_prev))
    def _():
        next_ref[...] = jnp.zeros_like(next_ref)

    @pl.when(jnp.logical_not(has_next))
    def _():
        prev_ref[...] = jnp.zeros_like(prev_ref)

    t_copy.wait()
    wg_ref[...] = wg_ref[...] + terms[pl.ds(pl.multiple_of(core * shard, 64), shard), :]

    @pl.when(has_next)
    def _():
        for g in range(kv_heads):
            next_copy(g).wait_send()
        for k in range(chips):
            ig_copies[k].wait_recv()

    @pl.when(has_prev)
    def _():
        for g in range(kv_heads):
            next_copy(g).wait_recv()
        for k in range(chips):
            ig_copies[k].wait_send()


def hand_over(*refs):
    sources, targets, sem = refs[:4], refs[4:8], refs[8]
    copies = [
        pltpu.make_async_copy(source, target, sem.at[i])
        for i, (source, target) in enumerate(zip(sources, targets))
    ]
    for copy in copies:
        copy.start()
    for copy in copies:
        copy.wait()


def fused_shards(chips, stages, fwd_x, fwd_q, bwd_x, bwd_q, bwd_dout, cache_kv, kv_weight, lengths):
    seg, model = fwd_x.shape[2:]
    seq_len, both = cache_kv.shape[2:]
    shard = kv_weight.shape[1]
    window = model // chips
    kv_heads = both // 2 // HD
    wide = pltpu.VMEM((seg, model), jnp.bfloat16)
    vmem, dma = pltpu.VMEM, pltpu.SemaphoreType.DMA
    bf16, f32 = jnp.bfloat16, jnp.float32
    outs = pl.pallas_call(
        functools.partial(fused, chips, stages),
        out_shape=(wide, wide, wide, pltpu.VMEM((shard, both), f32)),
        in_specs=[pl.BlockSpec(memory_space=pltpu.SMEM)] + [pl.BlockSpec(memory_space=pl.ANY)] * 7,
        out_specs=[pl.BlockSpec(memory_space=pltpu.VMEM)] * 4,
        scratch_shapes=[
            vmem((seq_len, both), bf16),
            vmem((seg, model), bf16),
            vmem((seg, model), bf16),
            vmem((seg, model), bf16),
            vmem((2 * shard, both), bf16),
            vmem((chips, seg, window), bf16),
            vmem((chips, seg, window), bf16),
            vmem((chips, seg, both), bf16),
            vmem((chips, seg, both), bf16),
            vmem((chips, seg, both), bf16),
            vmem((2 * seg, both), bf16),
            vmem((seg, model), bf16),
            vmem((chips, seg, window), bf16),
            vmem((2 * shard, both), f32),
            dma((7,)),
        ]
        + [dma((chips,))] * 10
        + [dma((kv_heads,)), dma((kv_heads,)), dma((2,)), dma((2,))],
        compiler_params=pltpu.CompilerParams(
            collective_id=0, has_side_effects=True, vmem_limit_bytes=59 * 1024 * 1024
        ),
    )(
        lengths,
        fwd_x[0, 0],
        fwd_q[0, 0],
        bwd_x[0, 0],
        bwd_q[0, 0],
        bwd_dout[0, 0],
        cache_kv[0, 0],
        kv_weight[0],
    )
    next_act, grad_query, prev_grad, weight_grad = pl.pallas_call(
        hand_over,
        out_shape=tuple(jax.ShapeDtypeStruct(out.shape, out.dtype) for out in outs),
        in_specs=[pl.BlockSpec(memory_space=pltpu.VMEM)] * 4,
        out_specs=[pl.BlockSpec(memory_space=pl.ANY)] * 4,
        scratch_shapes=[dma((4,))],
        compiler_params=pltpu.CompilerParams(vmem_limit_bytes=16 * 1024 * 1024),
    )(*outs)
    return (next_act[None, None], grad_query[None, None], prev_grad[None, None], weight_grad[None])


def solution(mesh):
    ranks, stages = mesh.shape["dp"], mesh.shape["pipe"]

    def body(fwd_x, *rest):
        if ranks % 2 == 0 and fwd_x.shape[-1] % (ranks // 2 * LANES) == 0:
            return fused_shards(ranks // 2, stages, fwd_x, *rest)
        return shards(fwd_x, *rest)

    return jax.shard_map(
        body,
        mesh=mesh,
        in_specs=(
            P("pipe", "dp", None, None),
            P("pipe", "dp", None, None),
            P("pipe", "dp", None, None),
            P("pipe", "dp", None, None),
            P("pipe", "dp", None, None),
            P("pipe", "dp", None, None),
            P("pipe", "dp", None),
            P("pipe", "dp", None),
        ),
        out_specs=(
            P("pipe", "dp", None, None),
            P("pipe", "dp", None, None),
            P("pipe", "dp", None, None),
            P("pipe", "dp", None),
        ),
        check_vma=False,
    )
```

```python
import functools
import math

import jax
import jax.numpy as jnp
from jax import lax
from jax.experimental import pallas as pl
from jax.experimental.pallas import tpu as pltpu
from jax.sharding import PartitionSpec as P

HD = 128


def shifted(value, axis, steps):
    count = lax.axis_size(axis)
    first, last = (max(0, -steps), min(count, count - steps))
    return lax.ppermute(value, axis, [(source, source + steps) for source in range(first, last)])


def masked_softmax(scores, allowed):
    masked = jnp.where(allowed[:, None, :], scores, -1e30)
    top = jnp.max(masked, axis=-1, keepdims=True)
    raised = jnp.exp(masked - top)
    return raised / jnp.sum(raised, axis=-1, keepdims=True)


def forward_segment(query, own_kv, cache, length):
    seg = query.shape[0]
    seq_len = cache.shape[0]
    half = cache.shape[1] // 2
    kv_heads = half // HD
    group = query.shape[1] // half
    scale = 1.0 / math.sqrt(HD)
    start = seq_len - length
    rows = jnp.arange(seg, dtype=jnp.int32)
    cache_ok = jnp.broadcast_to(
        jnp.arange(seq_len, dtype=jnp.int32)[None, :] < start, (seg, seq_len)
    )
    own_ok = (rows[None, :] <= rows[:, None]) & (rows[None, :] < length)
    allowed = jnp.concatenate([cache_ok, own_ok], axis=1)
    keys = jnp.concatenate([cache[:, :half], own_kv[:, :half]], axis=0)
    values = jnp.concatenate([cache[:, half:], own_kv[:, half:]], axis=0)
    pieces = []
    for head in range(kv_heads):
        block = query[:, head * group * HD : (head + 1) * group * HD].reshape(seg * group, HD)
        key_head = keys[:, head * HD : (head + 1) * HD]
        scores = (jnp.dot(block, key_head.T, preferred_element_type=jnp.float32) * scale).reshape(
            seg, group, -1
        )
        probs = masked_softmax(scores, allowed).astype(jnp.bfloat16).reshape(seg * group, -1)
        mixed = jnp.dot(
            probs, values[:, head * HD : (head + 1) * HD], preferred_element_type=jnp.float32
        )
        pieces.append(mixed.reshape(seg, group * HD))
    result = jnp.concatenate(pieces, axis=1)
    return jnp.where((rows < length)[:, None], result, 0.0).astype(jnp.bfloat16)


def backward_segment(query, dout, cache, third, fourth):
    seg = query.shape[0]
    seq_len = cache.shape[0]
    half = cache.shape[1] // 2
    kv_heads = half // HD
    group = query.shape[1] // half
    scale = 1.0 / math.sqrt(HD)
    start = seq_len - fourth - third
    rows = jnp.arange(seg, dtype=jnp.int32)
    allowed = jnp.arange(seq_len, dtype=jnp.int32)[None, :] <= start + rows[:, None]
    live = (rows < third)[:, None]
    dout = jnp.where(live, dout, jnp.zeros_like(dout))
    query_parts, key_parts, value_parts = ([], [], [])
    for head in range(kv_heads):
        block = query[:, head * group * HD : (head + 1) * group * HD].reshape(seg * group, HD)
        grad_block = dout[:, head * group * HD : (head + 1) * group * HD].reshape(seg * group, HD)
        key_head = cache[:, head * HD : (head + 1) * HD]
        value_head = cache[:, half + head * HD : half + (head + 1) * HD]
        scores = (jnp.dot(block, key_head.T, preferred_element_type=jnp.float32) * scale).reshape(
            seg, group, seq_len
        )
        probs = masked_softmax(scores, allowed).reshape(seg * group, seq_len)
        rounded = probs.astype(jnp.bfloat16)
        mixed = jnp.dot(rounded, value_head, preferred_element_type=jnp.float32)
        delta = jnp.sum(grad_block.astype(jnp.float32) * mixed, axis=1, keepdims=True)
        along = jnp.dot(grad_block, value_head.T, preferred_element_type=jnp.float32)
        dscore = (probs * (along - delta)).astype(jnp.bfloat16)
        query_parts.append(
            (jnp.dot(dscore, key_head, preferred_element_type=jnp.float32) * scale).reshape(
                seg, group * HD
            )
        )
        dscore_own = lax.dynamic_slice_in_dim(dscore, start, seg, 1)
        rounded_own = lax.dynamic_slice_in_dim(rounded, start, seg, 1)
        key_parts.append(jnp.dot(dscore_own.T, block, preferred_element_type=jnp.float32) * scale)
        value_parts.append(jnp.dot(rounded_own.T, grad_block, preferred_element_type=jnp.float32))
    grad_query = jnp.concatenate(query_parts, axis=1).astype(jnp.bfloat16)
    kv_grad = jnp.concatenate(key_parts + value_parts, axis=1)
    kv_grad = jnp.where(live, kv_grad, 0.0).astype(jnp.bfloat16)
    return (grad_query, kv_grad)


def shards(fwd_x, fwd_q, bwd_x, bwd_q, bwd_dout, cache_kv, kv_weight, seg_lengths):
    front_x = fwd_x[0, 0]
    front_q = fwd_q[0, 0]
    back_x = bwd_x[0, 0]
    back_q = bwd_q[0, 0]
    back_dout = bwd_dout[0, 0]
    cache = cache_kv[0, 0]
    shard = kv_weight[0]
    lengths = seg_lengths[0, 0]
    columns = front_x
    own_kv = jnp.dot(
        columns, lax.all_gather(shard, "dp", axis=0, tiled=True), preferred_element_type=jnp.float32
    ).astype(jnp.bfloat16)
    fwd_out = forward_segment(front_q, own_kv, cache, lengths[3])
    grad_query, kv_grad = backward_segment(back_q, back_dout, cache, lengths[2], lengths[3])
    input_grad = jnp.dot(
        kv_grad,
        lax.all_gather(shard, "dp", axis=0, tiled=True).T,
        preferred_element_type=jnp.float32,
    ).astype(jnp.bfloat16)
    columns = back_x
    weight_grad = lax.psum_scatter(
        jnp.dot(columns.T, kv_grad, preferred_element_type=jnp.float32),
        "dp",
        scatter_dimension=0,
        tiled=True,
    )
    next_act = shifted(fwd_out, "pipe", 1)
    prev_grad = shifted(input_grad, "pipe", -1)
    return (next_act[None, None], grad_query[None, None], prev_grad[None, None], weight_grad[None])

MESH = pl.DeviceIdType.MESH
LANES = 128
LOG2E = math.log2(math.e)


def dot(a, b, dims):
    return lax.dot_general(a, b, (dims, ((), ())), preferred_element_type=jnp.float32)


def heads_of(ref, g, group):
    width = group * HD
    columns = ref[:, pl.ds(g * width, width)]
    return jnp.concatenate([columns[:, h * HD : (h + 1) * HD] for h in range(group)], axis=0)


def heads_back(value, group):
    seg = value.shape[0] // group
    return jnp.concatenate([value[h * seg : (h + 1) * seg] for h in range(group)], axis=1)


def fused(
    chips,
    stages,
    len_ref,
    fx_ref,
    fq_ref,
    bx_ref,
    bq_ref,
    bd_ref,
    cache_ref,
    w_ref,
    next_ref,
    gq_ref,
    prev_ref,
    wg_ref,
    cache,
    bq,
    bd,
    fq,
    weight,
    xf,
    xb,
    part,
    own_in,
    kg,
    high,
    fout,
    igrad,
    terms,
    load_sem,
    xf_s,
    xf_r,
    xb_s,
    xb_r,
    own_s,
    own_r,
    kg_s,
    kg_r,
    ig_s,
    ig_r,
    na_s,
    na_r,
    pair_s,
    pair_r,
):
    seg, model = bq.shape
    seq_len, both = cache.shape
    half = both // 2
    kv_heads = half // HD
    group = model // half
    window = model // chips
    shard = w_ref.shape[0]
    width = group * HD
    low = seq_len - 2 * seg
    scale = 1.0 / math.sqrt(HD)
    me = lax.axis_index("dp")
    stage = lax.axis_index("pipe")
    chip, core = me // 2, me % 2
    has_next, has_prev = stage < stages - 1, stage > 0

    def at_chip(k):
        return ((chip + k) % chips) * 2 + core

    def columns_of(index):
        return pl.ds(pl.multiple_of(index * window, LANES), window)

    loads = [
        pltpu.make_async_copy(source, target, load_sem.at[i])
        for i, (source, target) in enumerate(
            [
                (bq_ref, bq),
                (cache_ref, cache),
                (bd_ref, bd),
                (fx_ref.at[:, columns_of(chip)], xf.at[0]),
                (w_ref, weight.at[pl.ds(pl.multiple_of(core * shard, 64), shard)]),
                (fq_ref, fq),
                (bx_ref.at[:, columns_of(chip)], xb.at[0]),
            ]
        )
    ]
    for load in loads:
        load.start()

    barrier = pltpu.get_barrier_semaphore()
    sibling = chip * 2 + 1 - core
    pl.semaphore_signal(barrier, inc=1, device_id={"dp": sibling}, device_id_type=MESH)
    for k in range(1, chips):
        pl.semaphore_signal(barrier, inc=1, device_id={"dp": at_chip(k)}, device_id_type=MESH)

    @pl.when(has_next)
    def _():
        for k in range(chips):
            pl.semaphore_signal(
                barrier, inc=1, device_id={"dp": at_chip(k), "pipe": stage + 1}, device_id_type=MESH
            )

    @pl.when(has_prev)
    def _():
        for k in range(chips):
            pl.semaphore_signal(
                barrier, inc=1, device_id={"dp": at_chip(k), "pipe": stage - 1}, device_id_type=MESH
            )

    sides = (stage + stages - 1) // stages + (2 * stages - 2 - stage) // stages
    pl.semaphore_wait(barrier, chips * (1 + sides))

    def remote(source, target, send, recv, device):
        return pltpu.make_async_remote_copy(
            src_ref=source,
            dst_ref=target,
            send_sem=send,
            recv_sem=recv,
            device_id=device,
            device_id_type=MESH,
        )

    def columns_copy(x_ref, slots, send, recv, k):
        there = (chip + k) % chips
        return remote(
            x_ref.at[:, columns_of(there)], slots.at[k], send.at[k], recv.at[k], {"dp": at_chip(k)}
        )

    xf_copies = [columns_copy(fx_ref, xf, xf_s, xf_r, k) for k in range(1, chips)]
    xb_copies = [columns_copy(bx_ref, xb, xb_s, xb_r, k) for k in range(1, chips)]
    w_copy = remote(
        w_ref,
        weight.at[pl.ds(pl.multiple_of(core * shard, 64), shard)],
        pair_s.at[0],
        pair_r.at[0],
        {"dp": sibling},
    )
    own_copies = [
        remote(part.at[k], own_in.at[k], own_s.at[k], own_r.at[k], {"dp": at_chip(chips - k)})
        for k in range(1, chips)
    ]
    kg_copies = [
        remote(kg.at[0], kg.at[k], kg_s.at[k], kg_r.at[k], {"dp": at_chip(k)})
        for k in range(1, chips)
    ]

    def kg_piece(k, piece):
        return remote(
            kg.at[0, :, piece], kg.at[k, :, piece], kg_s.at[k], kg_r.at[k], {"dp": at_chip(k)}
        )

    ig_copies = [
        remote(
            igrad.at[k],
            prev_ref.at[:, columns_of(chip)],
            ig_s.at[k],
            ig_r.at[k],
            {"dp": at_chip(chips - k), "pipe": stage - 1},
        )
        for k in range(chips)
    ]

    def next_copy(g):
        piece = pl.ds(g * width, width)
        return remote(
            fout.at[:, piece],
            next_ref.at[:, piece],
            na_s.at[g],
            na_r.at[g],
            {"dp": me, "pipe": stage + 1},
        )

    for copy in xf_copies:
        copy.start()
    w_copy.start()

    third, fourth = len_ref[0, 0, 2], len_ref[0, 0, 3]
    start3 = seq_len - fourth
    start2 = start3 - third
    row = lax.broadcasted_iota(jnp.int32, (seg, 1), 0)
    live2 = jnp.where(row < third, 1.0, 0.0)
    live3 = jnp.where(row < fourth, 1.0, 0.0)
    column = lax.broadcasted_iota(jnp.int32, (seg, seq_len - low), 1) + low
    row_wide = lax.broadcasted_iota(jnp.int32, (seg, seq_len - low), 0)

    def bias(start):
        piece = jnp.where(column <= start + row_wide, 0.0, -1e30)
        return jnp.concatenate([piece] * group, axis=0)

    def softmax_parts(scores_low, scores_high, start):
        scores_high = scores_high + bias(start)
        top = jnp.maximum(
            jnp.max(scores_low, axis=1, keepdims=True), jnp.max(scores_high, axis=1, keepdims=True)
        )
        raised_low = jnp.exp2((scores_low - top) * (scale * LOG2E))
        raised_high = jnp.exp2((scores_high - top) * (scale * LOG2E))
        total = jnp.sum(raised_low, axis=1, keepdims=True) + jnp.sum(
            raised_high, axis=1, keepdims=True
        )
        return raised_low, raised_high, 1.0 / total

    def lanes(start):
        return pl.ds(start, HD)

    def project():
        loads[3].wait()
        loads[4].wait()
        w_copy.wait()
        for copy in xf_copies:
            copy.wait()
        product = dot(xf[...].reshape(chips * seg, window), weight[...], ((1,), (0,)))
        part[...] = product.astype(jnp.bfloat16).reshape(part.shape)
        for copy in own_copies:
            copy.start()

    loads[0].wait()
    loads[1].wait()
    loads[2].wait()

    pick = (column == start2 + row_wide) & (row_wide < third)
    pick = jnp.where(pick, 1.0, 0.0).astype(jnp.bfloat16)

    def forward_begin(g):
        query = heads_of(fq, g, group)
        return query, dot(query, cache[:low, lanes(g * HD)], ((1,), (1,)))

    def forward_end(g, query, s_low):
        s_high = dot(query, high[:, lanes(g * HD)], ((1,), (1,)))
        e_low, e_high, inverse = softmax_parts(s_low, s_high, start3)
        mixed = dot(e_low.astype(jnp.bfloat16), cache[:low, lanes(half + g * HD)], ((1,), (0,)))
        mixed = mixed + dot(
            e_high.astype(jnp.bfloat16), high[:, lanes(half + g * HD)], ((1,), (0,))
        )
        mixed = mixed * (inverse * jnp.concatenate([live3] * group, axis=0))
        fout[:, pl.ds(g * width, width)] = heads_back(mixed, group).astype(jnp.bfloat16)

        @pl.when(has_next)
        def _():
            next_copy(g).start()

    def backward_begin(g):
        query = heads_of(bq, g, group)
        dout = heads_of(bd, g, group).astype(jnp.float32)
        dout = (dout * jnp.concatenate([live2] * group, axis=0)).astype(jnp.bfloat16)
        scores = dot(query, cache[:, lanes(g * HD)], ((1,), (1,)))
        along = dot(dout, cache[:, lanes(half + g * HD)], ((1,), (1,)))
        return query, dout, scores, along

    def backward_end(g, query, dout, scores, along):
        e_low, e_high, inverse = softmax_parts(scores[:, :low], scores[:, low:], start2)
        delta = jnp.sum(e_low * along[:, :low], axis=1, keepdims=True)
        delta = delta + jnp.sum(e_high * along[:, low:], axis=1, keepdims=True)
        delta = delta * inverse
        d_low = e_low * (along[:, :low] - delta)
        d_high = e_high * (along[:, low:] - delta)
        key_grad = dot((d_high * inverse).astype(jnp.bfloat16), query, ((0,), (0,))) * scale
        value_grad = dot((e_high * inverse).astype(jnp.bfloat16), dout, ((0,), (0,)))
        for start, part_grad in ((g * HD, key_grad), (half + g * HD, value_grad)):
            kg[0, :, lanes(start)] = dot(
                pick, part_grad.astype(jnp.bfloat16), ((1,), (0,))
            ).astype(jnp.bfloat16)
        for k in range(1, chips):
            kg_piece(k, lanes(g * HD)).start()
            kg_piece(k, lanes(half + g * HD)).start()
        keys = cache[:, lanes(g * HD)]
        grad = dot(d_low.astype(jnp.bfloat16), keys[:low], ((1,), (0,)))
        grad = grad + dot(d_high.astype(jnp.bfloat16), keys[low:], ((1,), (0,)))
        grad = grad * (inverse * scale)
        gq_ref[:, pl.ds(g * width, width)] = heads_back(grad, group).astype(jnp.bfloat16)

    loads[5].wait()
    state = backward_begin(0)
    for g in range(kv_heads):
        later = backward_begin(g + 1) if g + 1 < kv_heads else forward_begin(0)
        backward_end(g, *state)
        state = later
        if g == kv_heads // 2 - 1:
            project()

    t_copy = remote(
        terms.at[pl.ds(pl.multiple_of((1 - core) * shard, 64), shard)],
        wg_ref,
        pair_s.at[1],
        pair_r.at[1],
        {"dp": sibling},
    )

    def input_gradient(first, count):
        @pl.when(has_prev)
        def _():
            held = kg[first : first + count].reshape(count * seg, both)
            grad = dot(held, weight[...], ((1,), (1,))).astype(jnp.bfloat16)
            igrad[first : first + count] = grad.reshape(count, seg, window)
            for copy in ig_copies[first : first + count]:
                copy.start()

    def weight_terms():
        loads[6].wait()
        for copy in xb_copies:
            copy.wait()
        gathered = kg[...].reshape(chips * seg, both)
        terms[...] = dot(xb[...].reshape(chips * seg, window), gathered, ((0,), (0,)))
        t_copy.start()

    input_gradient(0, 1)
    for copy in kg_copies:
        copy.wait()
    input_gradient(1, chips - 1)
    for copy in xb_copies:
        copy.start()

    for copy in own_copies:
        copy.wait()
    own = part[0].astype(jnp.float32)
    for k in range(1, chips):
        own = own + own_in[k].astype(jnp.float32)
    own = own.astype(jnp.bfloat16)
    spot = lax.broadcasted_iota(jnp.int32, (seq_len - low, seg), 0) + low
    source = lax.broadcasted_iota(jnp.int32, (seq_len - low, seg), 1)
    place = jnp.where(spot == start3 + source, 1.0, 0.0).astype(jnp.bfloat16)
    moved = dot(place, own, ((1,), (0,)))
    stored = lax.broadcasted_iota(jnp.int32, (seq_len - low, both), 0) + low < start3
    high[...] = jnp.where(stored, cache[low:, :].astype(jnp.float32), moved).astype(jnp.bfloat16)

    for g in range(kv_heads):
        later = forward_begin(g + 1) if g + 1 < kv_heads else None
        forward_end(g, *state)
        state = later
        if g == kv_heads - 2:
            weight_terms()

    @pl.when(jnp.logical_not(has_prev))
    def _():
        next_ref[...] = jnp.zeros_like(next_ref)

    @pl.when(jnp.logical_not(has_next))
    def _():
        prev_ref[...] = jnp.zeros_like(prev_ref)

    t_copy.wait()
    wg_ref[...] = wg_ref[...] + terms[pl.ds(pl.multiple_of(core * shard, 64), shard), :]

    @pl.when(has_next)
    def _():
        for g in range(kv_heads):
            next_copy(g).wait_send()
        for k in range(chips):
            ig_copies[k].wait_recv()

    @pl.when(has_prev)
    def _():
        for g in range(kv_heads):
            next_copy(g).wait_recv()
        for k in range(chips):
            ig_copies[k].wait_send()


def hand_over(*refs):
    sources, targets, sem = refs[:4], refs[4:8], refs[8]
    copies = [
        pltpu.make_async_copy(source, target, sem.at[i])
        for i, (source, target) in enumerate(zip(sources, targets))
    ]
    for copy in copies:
        copy.start()
    for copy in copies:
        copy.wait()


def fused_shards(chips, stages, fwd_x, fwd_q, bwd_x, bwd_q, bwd_dout, cache_kv, kv_weight, lengths):
    seg, model = fwd_x.shape[2:]
    seq_len, both = cache_kv.shape[2:]
    shard = kv_weight.shape[1]
    window = model // chips
    kv_heads = both // 2 // HD
    wide = pltpu.VMEM((seg, model), jnp.bfloat16)
    vmem, dma = pltpu.VMEM, pltpu.SemaphoreType.DMA
    bf16, f32 = jnp.bfloat16, jnp.float32
    outs = pl.pallas_call(
        functools.partial(fused, chips, stages),
        out_shape=(wide, wide, wide, pltpu.VMEM((shard, both), f32)),
        in_specs=[pl.BlockSpec(memory_space=pltpu.SMEM)] + [pl.BlockSpec(memory_space=pl.ANY)] * 7,
        out_specs=[pl.BlockSpec(memory_space=pltpu.VMEM)] * 4,
        scratch_shapes=[
            vmem((seq_len, both), bf16),
            vmem((seg, model), bf16),
            vmem((seg, model), bf16),
            vmem((seg, model), bf16),
            vmem((2 * shard, both), bf16),
            vmem((chips, seg, window), bf16),
            vmem((chips, seg, window), bf16),
            vmem((chips, seg, both), bf16),
            vmem((chips, seg, both), bf16),
            vmem((chips, seg, both), bf16),
            vmem((2 * seg, both), bf16),
            vmem((seg, model), bf16),
            vmem((chips, seg, window), bf16),
            vmem((2 * shard, both), f32),
            dma((7,)),
        ]
        + [dma((chips,))] * 10
        + [dma((kv_heads,)), dma((kv_heads,)), dma((2,)), dma((2,))],
        compiler_params=pltpu.CompilerParams(
            collective_id=0, has_side_effects=True, vmem_limit_bytes=59 * 1024 * 1024
        ),
    )(
        lengths,
        fwd_x[0, 0],
        fwd_q[0, 0],
        bwd_x[0, 0],
        bwd_q[0, 0],
        bwd_dout[0, 0],
        cache_kv[0, 0],
        kv_weight[0],
    )
    next_act, grad_query, prev_grad, weight_grad = pl.pallas_call(
        hand_over,
        out_shape=tuple(jax.ShapeDtypeStruct(out.shape, out.dtype) for out in outs),
        in_specs=[pl.BlockSpec(memory_space=pltpu.VMEM)] * 4,
        out_specs=[pl.BlockSpec(memory_space=pl.ANY)] * 4,
        scratch_shapes=[dma((4,))],
        compiler_params=pltpu.CompilerParams(vmem_limit_bytes=16 * 1024 * 1024),
    )(*outs)
    return (next_act[None, None], grad_query[None, None], prev_grad[None, None], weight_grad[None])


def solution(mesh):
    ranks, stages = mesh.shape["dp"], mesh.shape["pipe"]

    def body(fwd_x, *rest):
        if ranks % 2 == 0 and fwd_x.shape[-1] % (ranks // 2 * LANES) == 0:
            return fused_shards(ranks // 2, stages, fwd_x, *rest)
        return shards(fwd_x, *rest)

    return jax.shard_map(
        body,
        mesh=mesh,
        in_specs=(
            P("pipe", "dp", None, None),
            P("pipe", "dp", None, None),
            P("pipe", "dp", None, None),
            P("pipe", "dp", None, None),
            P("pipe", "dp", None, None),
            P("pipe", "dp", None, None),
            P("pipe", "dp", None),
            P("pipe", "dp", None),
        ),
        out_specs=(
            P("pipe", "dp", None, None),
            P("pipe", "dp", None, None),
            P("pipe", "dp", None, None),
            P("pipe", "dp", None),
        ),
        check_vma=False,
    )
```

```python
import functools
import math

import jax
import jax.numpy as jnp
from jax import lax
from jax.experimental import pallas as pl
from jax.experimental.pallas import tpu as pltpu
from jax.sharding import PartitionSpec as P

HD = 128


def shifted(value, axis, steps):
    count = lax.axis_size(axis)
    first, last = (max(0, -steps), min(count, count - steps))
    return lax.ppermute(value, axis, [(source, source + steps) for source in range(first, last)])


def masked_softmax(scores, allowed):
    masked = jnp.where(allowed[:, None, :], scores, -1e30)
    top = jnp.max(masked, axis=-1, keepdims=True)
    raised = jnp.exp(masked - top)
    return raised / jnp.sum(raised, axis=-1, keepdims=True)


def forward_segment(query, own_kv, cache, length):
    seg = query.shape[0]
    seq_len = cache.shape[0]
    half = cache.shape[1] // 2
    kv_heads = half // HD
    group = query.shape[1] // half
    scale = 1.0 / math.sqrt(HD)
    start = seq_len - length
    rows = jnp.arange(seg, dtype=jnp.int32)
    cache_ok = jnp.broadcast_to(
        jnp.arange(seq_len, dtype=jnp.int32)[None, :] < start, (seg, seq_len)
    )
    own_ok = (rows[None, :] <= rows[:, None]) & (rows[None, :] < length)
    allowed = jnp.concatenate([cache_ok, own_ok], axis=1)
    keys = jnp.concatenate([cache[:, :half], own_kv[:, :half]], axis=0)
    values = jnp.concatenate([cache[:, half:], own_kv[:, half:]], axis=0)
    pieces = []
    for head in range(kv_heads):
        block = query[:, head * group * HD : (head + 1) * group * HD].reshape(seg * group, HD)
        key_head = keys[:, head * HD : (head + 1) * HD]
        scores = (jnp.dot(block, key_head.T, preferred_element_type=jnp.float32) * scale).reshape(
            seg, group, -1
        )
        probs = masked_softmax(scores, allowed).astype(jnp.bfloat16).reshape(seg * group, -1)
        mixed = jnp.dot(
            probs, values[:, head * HD : (head + 1) * HD], preferred_element_type=jnp.float32
        )
        pieces.append(mixed.reshape(seg, group * HD))
    result = jnp.concatenate(pieces, axis=1)
    return jnp.where((rows < length)[:, None], result, 0.0).astype(jnp.bfloat16)


def backward_segment(query, dout, cache, third, fourth):
    seg = query.shape[0]
    seq_len = cache.shape[0]
    half = cache.shape[1] // 2
    kv_heads = half // HD
    group = query.shape[1] // half
    scale = 1.0 / math.sqrt(HD)
    start = seq_len - fourth - third
    rows = jnp.arange(seg, dtype=jnp.int32)
    allowed = jnp.arange(seq_len, dtype=jnp.int32)[None, :] <= start + rows[:, None]
    live = (rows < third)[:, None]
    dout = jnp.where(live, dout, jnp.zeros_like(dout))
    query_parts, key_parts, value_parts = ([], [], [])
    for head in range(kv_heads):
        block = query[:, head * group * HD : (head + 1) * group * HD].reshape(seg * group, HD)
        grad_block = dout[:, head * group * HD : (head + 1) * group * HD].reshape(seg * group, HD)
        key_head = cache[:, head * HD : (head + 1) * HD]
        value_head = cache[:, half + head * HD : half + (head + 1) * HD]
        scores = (jnp.dot(block, key_head.T, preferred_element_type=jnp.float32) * scale).reshape(
            seg, group, seq_len
        )
        probs = masked_softmax(scores, allowed).reshape(seg * group, seq_len)
        rounded = probs.astype(jnp.bfloat16)
        mixed = jnp.dot(rounded, value_head, preferred_element_type=jnp.float32)
        delta = jnp.sum(grad_block.astype(jnp.float32) * mixed, axis=1, keepdims=True)
        along = jnp.dot(grad_block, value_head.T, preferred_element_type=jnp.float32)
        dscore = (probs * (along - delta)).astype(jnp.bfloat16)
        query_parts.append(
            (jnp.dot(dscore, key_head, preferred_element_type=jnp.float32) * scale).reshape(
                seg, group * HD
            )
        )
        dscore_own = lax.dynamic_slice_in_dim(dscore, start, seg, 1)
        rounded_own = lax.dynamic_slice_in_dim(rounded, start, seg, 1)
        key_parts.append(jnp.dot(dscore_own.T, block, preferred_element_type=jnp.float32) * scale)
        value_parts.append(jnp.dot(rounded_own.T, grad_block, preferred_element_type=jnp.float32))
    grad_query = jnp.concatenate(query_parts, axis=1).astype(jnp.bfloat16)
    kv_grad = jnp.concatenate(key_parts + value_parts, axis=1)
    kv_grad = jnp.where(live, kv_grad, 0.0).astype(jnp.bfloat16)
    return (grad_query, kv_grad)


def shards(fwd_x, fwd_q, bwd_x, bwd_q, bwd_dout, cache_kv, kv_weight, seg_lengths):
    front_x = fwd_x[0, 0]
    front_q = fwd_q[0, 0]
    back_x = bwd_x[0, 0]
    back_q = bwd_q[0, 0]
    back_dout = bwd_dout[0, 0]
    cache = cache_kv[0, 0]
    shard = kv_weight[0]
    lengths = seg_lengths[0, 0]
    columns = front_x
    own_kv = jnp.dot(
        columns, lax.all_gather(shard, "dp", axis=0, tiled=True), preferred_element_type=jnp.float32
    ).astype(jnp.bfloat16)
    fwd_out = forward_segment(front_q, own_kv, cache, lengths[3])
    grad_query, kv_grad = backward_segment(back_q, back_dout, cache, lengths[2], lengths[3])
    input_grad = jnp.dot(
        kv_grad,
        lax.all_gather(shard, "dp", axis=0, tiled=True).T,
        preferred_element_type=jnp.float32,
    ).astype(jnp.bfloat16)
    columns = back_x
    weight_grad = lax.psum_scatter(
        jnp.dot(columns.T, kv_grad, preferred_element_type=jnp.float32),
        "dp",
        scatter_dimension=0,
        tiled=True,
    )
    next_act = shifted(fwd_out, "pipe", 1)
    prev_grad = shifted(input_grad, "pipe", -1)
    return (next_act[None, None], grad_query[None, None], prev_grad[None, None], weight_grad[None])

MESH = pl.DeviceIdType.MESH
LANES = 128
LOG2E = math.log2(math.e)


def dot(a, b, dims):
    return lax.dot_general(a, b, (dims, ((), ())), preferred_element_type=jnp.float32)


def heads_of(ref, g, group):
    width = group * HD
    columns = ref[:, pl.ds(g * width, width)]
    return jnp.concatenate([columns[:, h * HD : (h + 1) * HD] for h in range(group)], axis=0)


def heads_back(value, group):
    seg = value.shape[0] // group
    return jnp.concatenate([value[h * seg : (h + 1) * seg] for h in range(group)], axis=1)


def fused(
    chips,
    stages,
    len_ref,
    fx_ref,
    fq_ref,
    bx_ref,
    bq_ref,
    bd_ref,
    cache_ref,
    w_ref,
    next_ref,
    gq_ref,
    prev_ref,
    wg_ref,
    cache,
    bq,
    bd,
    fq,
    weight,
    xf,
    xb,
    part,
    own_in,
    kg,
    high,
    fout,
    igrad,
    terms,
    term_out,
    term_in,
    load_sem,
    xf_s,
    xf_r,
    xb_s,
    xb_r,
    own_s,
    own_r,
    kg_s,
    kg_r,
    ig_s,
    ig_r,
    na_s,
    na_r,
    pair_s,
    pair_r,
):
    seg, model = bq.shape
    seq_len, both = cache.shape
    half = both // 2
    kv_heads = half // HD
    group = model // half
    window = model // chips
    shard = w_ref.shape[0]
    width = group * HD
    low = seq_len - 2 * seg
    scale = 1.0 / math.sqrt(HD)
    me = lax.axis_index("dp")
    stage = lax.axis_index("pipe")
    chip, core = me // 2, me % 2
    has_next, has_prev = stage < stages - 1, stage > 0

    def at_chip(k):
        return ((chip + k) % chips) * 2 + core

    def columns_of(index):
        return pl.ds(pl.multiple_of(index * window, LANES), window)

    loads = [
        pltpu.make_async_copy(source, target, load_sem.at[i])
        for i, (source, target) in enumerate(
            [
                (bq_ref, bq),
                (cache_ref, cache),
                (bd_ref, bd),
                (fx_ref.at[:, columns_of(chip)], xf.at[0]),
                (w_ref, weight.at[pl.ds(pl.multiple_of(core * shard, 64), shard)]),
                (fq_ref, fq),
                (bx_ref.at[:, columns_of(chip)], xb.at[0]),
            ]
        )
    ]
    for load in loads:
        load.start()

    barrier = pltpu.get_barrier_semaphore()
    sibling = chip * 2 + 1 - core
    pl.semaphore_signal(barrier, inc=1, device_id={"dp": sibling}, device_id_type=MESH)
    for k in range(1, chips):
        pl.semaphore_signal(barrier, inc=1, device_id={"dp": at_chip(k)}, device_id_type=MESH)

    @pl.when(has_next)
    def _():
        for k in range(chips):
            pl.semaphore_signal(
                barrier, inc=1, device_id={"dp": at_chip(k), "pipe": stage + 1}, device_id_type=MESH
            )

    @pl.when(has_prev)
    def _():
        for k in range(chips):
            pl.semaphore_signal(
                barrier, inc=1, device_id={"dp": at_chip(k), "pipe": stage - 1}, device_id_type=MESH
            )

    sides = (stage + stages - 1) // stages + (2 * stages - 2 - stage) // stages
    pl.semaphore_wait(barrier, chips * (1 + sides))

    def remote(source, target, send, recv, device):
        return pltpu.make_async_remote_copy(
            src_ref=source,
            dst_ref=target,
            send_sem=send,
            recv_sem=recv,
            device_id=device,
            device_id_type=MESH,
        )

    def columns_copy(x_ref, slots, send, recv, k):
        there = (chip + k) % chips
        return remote(
            x_ref.at[:, columns_of(there)], slots.at[k], send.at[k], recv.at[k], {"dp": at_chip(k)}
        )

    xf_copies = [columns_copy(fx_ref, xf, xf_s, xf_r, k) for k in range(1, chips)]
    xb_copies = [columns_copy(bx_ref, xb, xb_s, xb_r, k) for k in range(1, chips)]
    w_copy = remote(
        w_ref,
        weight.at[pl.ds(pl.multiple_of(core * shard, 64), shard)],
        pair_s.at[0],
        pair_r.at[0],
        {"dp": sibling},
    )
    own_copies = [
        remote(part.at[k], own_in.at[k], own_s.at[k], own_r.at[k], {"dp": at_chip(chips - k)})
        for k in range(1, chips)
    ]
    kg_copies = [
        remote(kg.at[0], kg.at[k], kg_s.at[k], kg_r.at[k], {"dp": at_chip(k)})
        for k in range(1, chips)
    ]

    def kg_piece(k, piece):
        return remote(
            kg.at[0, :, piece], kg.at[k, :, piece], kg_s.at[k], kg_r.at[k], {"dp": at_chip(k)}
        )

    ig_copies = [
        remote(
            igrad.at[k],
            prev_ref.at[:, columns_of(chip)],
            ig_s.at[k],
            ig_r.at[k],
            {"dp": at_chip(chips - k), "pipe": stage - 1},
        )
        for k in range(chips)
    ]

    def next_copy(g):
        piece = pl.ds(g * width, width)
        return remote(
            fout.at[:, piece],
            next_ref.at[:, piece],
            na_s.at[g],
            na_r.at[g],
            {"dp": me, "pipe": stage + 1},
        )

    for copy in xf_copies:
        copy.start()
    w_copy.start()

    third, fourth = len_ref[0, 0, 2], len_ref[0, 0, 3]
    start3 = seq_len - fourth
    start2 = start3 - third
    row = lax.broadcasted_iota(jnp.int32, (seg, 1), 0)
    live2 = jnp.where(row < third, 1.0, 0.0)
    live3 = jnp.where(row < fourth, 1.0, 0.0)
    column = lax.broadcasted_iota(jnp.int32, (seg, seq_len - low), 1) + low
    row_wide = lax.broadcasted_iota(jnp.int32, (seg, seq_len - low), 0)

    def bias(start):
        piece = jnp.where(column <= start + row_wide, 0.0, -1e30)
        return jnp.concatenate([piece] * group, axis=0)

    def softmax_parts(scores_low, scores_high, start):
        scores_high = scores_high + bias(start)
        top = jnp.maximum(
            jnp.max(scores_low, axis=1, keepdims=True), jnp.max(scores_high, axis=1, keepdims=True)
        )
        raised_low = jnp.exp2((scores_low - top) * (scale * LOG2E))
        raised_high = jnp.exp2((scores_high - top) * (scale * LOG2E))
        total = jnp.sum(raised_low, axis=1, keepdims=True) + jnp.sum(
            raised_high, axis=1, keepdims=True
        )
        return raised_low, raised_high, 1.0 / total

    def lanes(start):
        return pl.ds(start, HD)

    def project():
        loads[3].wait()
        loads[4].wait()
        w_copy.wait()
        for copy in xf_copies:
            copy.wait()
        product = dot(xf[...].reshape(chips * seg, window), weight[...], ((1,), (0,)))
        part[...] = product.astype(jnp.bfloat16).reshape(part.shape)
        for copy in own_copies:
            copy.start()

    loads[0].wait()
    loads[1].wait()
    loads[2].wait()

    pick = (column == start2 + row_wide) & (row_wide < third)
    pick = jnp.where(pick, 1.0, 0.0).astype(jnp.bfloat16)

    def forward_begin(g):
        query = heads_of(fq, g, group)
        return query, dot(query, cache[:low, lanes(g * HD)], ((1,), (1,)))

    def forward_end(g, query, s_low):
        s_high = dot(query, high[:, lanes(g * HD)], ((1,), (1,)))
        e_low, e_high, inverse = softmax_parts(s_low, s_high, start3)
        mixed = dot(e_low.astype(jnp.bfloat16), cache[:low, lanes(half + g * HD)], ((1,), (0,)))
        mixed = mixed + dot(
            e_high.astype(jnp.bfloat16), high[:, lanes(half + g * HD)], ((1,), (0,))
        )
        mixed = mixed * (inverse * jnp.concatenate([live3] * group, axis=0))
        fout[:, pl.ds(g * width, width)] = heads_back(mixed, group).astype(jnp.bfloat16)

        @pl.when(has_next)
        def _():
            next_copy(g).start()

    def backward_begin(g):
        query = heads_of(bq, g, group)
        dout = heads_of(bd, g, group).astype(jnp.float32)
        dout = (dout * jnp.concatenate([live2] * group, axis=0)).astype(jnp.bfloat16)
        scores = dot(query, cache[:, lanes(g * HD)], ((1,), (1,)))
        along = dot(dout, cache[:, lanes(half + g * HD)], ((1,), (1,)))
        return query, dout, scores, along

    def backward_end(g, query, dout, scores, along):
        e_low, e_high, inverse = softmax_parts(scores[:, :low], scores[:, low:], start2)
        delta = jnp.sum(e_low * along[:, :low], axis=1, keepdims=True)
        delta = delta + jnp.sum(e_high * along[:, low:], axis=1, keepdims=True)
        delta = delta * inverse
        d_low = e_low * (along[:, :low] - delta)
        d_high = e_high * (along[:, low:] - delta)
        key_grad = dot((d_high * inverse).astype(jnp.bfloat16), query, ((0,), (0,))) * scale
        value_grad = dot((e_high * inverse).astype(jnp.bfloat16), dout, ((0,), (0,)))
        for start, part_grad in ((g * HD, key_grad), (half + g * HD, value_grad)):
            kg[0, :, lanes(start)] = dot(
                pick, part_grad.astype(jnp.bfloat16), ((1,), (0,))
            ).astype(jnp.bfloat16)
        for k in range(1, chips):
            kg_piece(k, lanes(g * HD)).start()
            kg_piece(k, lanes(half + g * HD)).start()
        keys = cache[:, lanes(g * HD)]
        grad = dot(d_low.astype(jnp.bfloat16), keys[:low], ((1,), (0,)))
        grad = grad + dot(d_high.astype(jnp.bfloat16), keys[low:], ((1,), (0,)))
        grad = grad * (inverse * scale)
        gq_ref[:, pl.ds(g * width, width)] = heads_back(grad, group).astype(jnp.bfloat16)

    loads[5].wait()
    state = backward_begin(0)
    for g in range(kv_heads):
        later = backward_begin(g + 1) if g + 1 < kv_heads else forward_begin(0)
        backward_end(g, *state)
        state = later
        if g == kv_heads // 2 - 1:
            project()
            for copy in xb_copies:
                copy.start()

    t_copy = remote(
        term_out,
        term_in,
        pair_s.at[1],
        pair_r.at[1],
        {"dp": sibling},
    )

    def input_gradient(first, count):
        @pl.when(has_prev)
        def _():
            held = kg[first : first + count].reshape(count * seg, both)
            grad = dot(held, weight[...], ((1,), (1,))).astype(jnp.bfloat16)
            igrad[first : first + count] = grad.reshape(count, seg, window)
            for copy in ig_copies[first : first + count]:
                copy.start()

    def weight_terms():
        loads[6].wait()
        for copy in xb_copies:
            copy.wait()
        gathered = kg[...].reshape(chips * seg, both)
        terms[...] = dot(xb[...].reshape(chips * seg, window), gathered, ((0,), (0,)))
        theirs = terms[pl.ds(pl.multiple_of((1 - core) * shard, 64), shard), :]
        term_out[...] = theirs.astype(jnp.bfloat16)
        t_copy.start()

    input_gradient(0, 1)
    for copy in kg_copies:
        copy.wait()
    input_gradient(1, chips - 1)

    for copy in own_copies:
        copy.wait()
    own = part[0].astype(jnp.float32)
    for k in range(1, chips):
        own = own + own_in[k].astype(jnp.float32)
    own = own.astype(jnp.bfloat16)
    spot = lax.broadcasted_iota(jnp.int32, (seq_len - low, seg), 0) + low
    source = lax.broadcasted_iota(jnp.int32, (seq_len - low, seg), 1)
    place = jnp.where(spot == start3 + source, 1.0, 0.0).astype(jnp.bfloat16)
    moved = dot(place, own, ((1,), (0,)))
    stored = lax.broadcasted_iota(jnp.int32, (seq_len - low, both), 0) + low < start3
    high[...] = jnp.where(stored, cache[low:, :].astype(jnp.float32), moved).astype(jnp.bfloat16)

    for g in range(kv_heads):
        later = forward_begin(g + 1) if g + 1 < kv_heads else None
        forward_end(g, *state)
        state = later
        if g == 0:
            weight_terms()

    @pl.when(jnp.logical_not(has_prev))
    def _():
        next_ref[...] = jnp.zeros_like(next_ref)

    @pl.when(jnp.logical_not(has_next))
    def _():
        prev_ref[...] = jnp.zeros_like(prev_ref)

    t_copy.wait()
    mine = terms[pl.ds(pl.multiple_of(core * shard, 64), shard), :]
    wg_ref[...] = mine + term_in[...].astype(jnp.float32)

    @pl.when(has_next)
    def _():
        for g in range(kv_heads):
            next_copy(g).wait_send()
        for k in range(chips):
            ig_copies[k].wait_recv()

    @pl.when(has_prev)
    def _():
        for g in range(kv_heads):
            next_copy(g).wait_recv()
        for k in range(chips):
            ig_copies[k].wait_send()


def hand_over(*refs):
    sources, targets, sem = refs[:4], refs[4:8], refs[8]
    copies = [
        pltpu.make_async_copy(source, target, sem.at[i])
        for i, (source, target) in enumerate(zip(sources, targets))
    ]
    for copy in copies:
        copy.start()
    for copy in copies:
        copy.wait()


def fused_shards(chips, stages, fwd_x, fwd_q, bwd_x, bwd_q, bwd_dout, cache_kv, kv_weight, lengths):
    seg, model = fwd_x.shape[2:]
    seq_len, both = cache_kv.shape[2:]
    shard = kv_weight.shape[1]
    window = model // chips
    kv_heads = both // 2 // HD
    wide = pltpu.VMEM((seg, model), jnp.bfloat16)
    vmem, dma = pltpu.VMEM, pltpu.SemaphoreType.DMA
    bf16, f32 = jnp.bfloat16, jnp.float32
    outs = pl.pallas_call(
        functools.partial(fused, chips, stages),
        out_shape=(wide, wide, wide, pltpu.VMEM((shard, both), f32)),
        in_specs=[pl.BlockSpec(memory_space=pltpu.SMEM)] + [pl.BlockSpec(memory_space=pl.ANY)] * 7,
        out_specs=[pl.BlockSpec(memory_space=pltpu.VMEM)] * 4,
        scratch_shapes=[
            vmem((seq_len, both), bf16),
            vmem((seg, model), bf16),
            vmem((seg, model), bf16),
            vmem((seg, model), bf16),
            vmem((2 * shard, both), bf16),
            vmem((chips, seg, window), bf16),
            vmem((chips, seg, window), bf16),
            vmem((chips, seg, both), bf16),
            vmem((chips, seg, both), bf16),
            vmem((chips, seg, both), bf16),
            vmem((2 * seg, both), bf16),
            vmem((seg, model), bf16),
            vmem((chips, seg, window), bf16),
            vmem((2 * shard, both), f32),
            vmem((shard, both), bf16),
            vmem((shard, both), bf16),
            dma((7,)),
        ]
        + [dma((chips,))] * 10
        + [dma((kv_heads,)), dma((kv_heads,)), dma((2,)), dma((2,))],
        compiler_params=pltpu.CompilerParams(
            collective_id=0, has_side_effects=True, vmem_limit_bytes=59 * 1024 * 1024
        ),
    )(
        lengths,
        fwd_x[0, 0],
        fwd_q[0, 0],
        bwd_x[0, 0],
        bwd_q[0, 0],
        bwd_dout[0, 0],
        cache_kv[0, 0],
        kv_weight[0],
    )
    next_act, grad_query, prev_grad, weight_grad = pl.pallas_call(
        hand_over,
        out_shape=tuple(jax.ShapeDtypeStruct(out.shape, out.dtype) for out in outs),
        in_specs=[pl.BlockSpec(memory_space=pltpu.VMEM)] * 4,
        out_specs=[pl.BlockSpec(memory_space=pl.ANY)] * 4,
        scratch_shapes=[dma((4,))],
        compiler_params=pltpu.CompilerParams(vmem_limit_bytes=16 * 1024 * 1024),
    )(*outs)
    return (next_act[None, None], grad_query[None, None], prev_grad[None, None], weight_grad[None])


def solution(mesh):
    ranks, stages = mesh.shape["dp"], mesh.shape["pipe"]

    def body(fwd_x, *rest):
        if ranks % 2 == 0 and fwd_x.shape[-1] % (ranks // 2 * LANES) == 0:
            return fused_shards(ranks // 2, stages, fwd_x, *rest)
        return shards(fwd_x, *rest)

    return jax.shard_map(
        body,
        mesh=mesh,
        in_specs=(
            P("pipe", "dp", None, None),
            P("pipe", "dp", None, None),
            P("pipe", "dp", None, None),
            P("pipe", "dp", None, None),
            P("pipe", "dp", None, None),
            P("pipe", "dp", None, None),
            P("pipe", "dp", None),
            P("pipe", "dp", None),
        ),
        out_specs=(
            P("pipe", "dp", None, None),
            P("pipe", "dp", None, None),
            P("pipe", "dp", None, None),
            P("pipe", "dp", None),
        ),
        check_vma=False,
    )
```
